128 devices in a mesh: dp: 8 (over x_lo, z), seq: 16 (over x_hi, y, core).
Axes of the slice: x: 4 (x_hi: 2, x_lo: 2; x = x_hi * 2 + x_lo), y: 4, z: 4, core: 2. Of those that a mesh axis runs over, the one named last changes fastest.
Arguments:
- hidden: bfloat16 [8, 2048, 1024], P('dp', 'seq'), may hold values from -6 to 6
- cotangent: bfloat16 [8, 2048, 1024], P('dp', 'seq'), may hold values from -6 to 6
- segments: int32 [8, 2048], P('dp', 'seq'), may hold values from 0 to 4, as said below
- w_qkv: float32 [1024, 4096], P('seq'), may hold values from -0.1875 to 0.1875
- w_gu: float32 [1024, 6144], P('seq'), may hold values from -0.1875 to 0.1875
- w_o: float32 [2048, 1024], P('seq'), may hold values from -1.5 to 1.5
- w_down: float32 [3072, 1024], P('seq'), may hold values from -0.109375 to 0.109375
- norm_gains: float32 [2304], P('seq'), may hold values from 0.5 to 1.5
- m_qkv: float32 [1024, 4096], P('seq')
- m_gu: float32 [1024, 6144], P('seq')
- m_o: float32 [2048, 1024], P('seq')
- m_down: float32 [3072, 1024], P('seq')
- m_gains: float32 [2304], P('seq')
- v_qkv: float32 [1024, 4096], P('seq'), as said below
- v_gu: float32 [1024, 6144], P('seq'), as said below
- v_o: float32 [2048, 1024], P('seq'), as said below
- v_down: float32 [3072, 1024], P('seq'), as said below
- v_gains: float32 [2304], P('seq'), as said below
Outputs:
- output: bfloat16 [8, 2048, 1024], P('dp', 'seq')
- hidden_grad: float32 [8, 2048, 1024], P('dp', 'seq')
- qkv_first: float32 [1024, 4096], P('seq')
- qkv_second: float32 [1024, 4096], P('seq')
- qkv_weight: float32 [1024, 4096], P('seq')
- gu_first: float32 [1024, 6144], P('seq')
- gu_second: float32 [1024, 6144], P('seq')
- gu_weight: float32 [1024, 6144], P('seq')
- o_first: float32 [2048, 1024], P('seq')
- o_second: float32 [2048, 1024], P('seq')
- o_weight: float32 [2048, 1024], P('seq')
- down_first: float32 [3072, 1024], P('seq')
- down_second: float32 [3072, 1024], P('seq')
- down_weight: float32 [3072, 1024], P('seq')
- gains_first: float32 [2304], P('seq')
- gains_second: float32 [2304], P('seq')
- gains_weight: float32 [2304], P('seq')
The draws below stay inside these ranges and needn't reach their ends.
Inputs may be any that keep to these rules, and one draw needn't show every extreme that they name: `segments`: in each sequence the document numbers start at 0 and rise by one at each new document; every document has 200 tokens or more; some sequence is a single document and some sequence holds five. `v_qkv`: entries are positive. `v_gu`: entries are positive. `v_o`: entries are positive. `v_down`: entries are positive. `v_gains`: entries are positive.
All inputs are finite; a program needn't handle non-finite values.
Results may differ from the reference program's by a relative error of at most 0.025.
Values may be sent and summed in bfloat16 or wider, within the bound.
No kernel may reach another device: no remote copies, remote signals or barrier semaphores. Data moves between devices by JAX's collectives and lax.ppermute only.
A program may use at most 256 MiB of HBM per device.

```python
import math
import jax
import jax.numpy as jnp
from jax import lax

D = 1024
H = 16
KVH = 8
HD = 128
FF = 3072
KEYS_SEEN = 512
MIN_DOC = 200
STEP = 10
QD = 2048
QKVD = 4096
SEQLEN = 2048
SEQS = 8
TOKENS = 16384


def first_moment(key, shape, factor):
    spread = factor * math.sqrt(TOKENS) / 9.0
    return jax.random.normal(key, shape, jnp.float32) * spread


def second_moment(key, shape, factor):
    level = factor * factor * TOKENS / 19.0
    return level * jnp.exp(jax.random.uniform(key, shape, jnp.float32, 0.0, math.log(4.0)))


def draw_segments(key, part):
    key = jax.random.fold_in(key, 1)
    key_count, key_whole, key_full, key_cut = jax.random.split(key, 4)
    order = jnp.arange(SEQS, dtype=jnp.int32)
    cuts = jax.random.randint(key_count, (SEQS,), 2, 5).astype(jnp.int32)
    whole = jax.random.randint(key_whole, (), 0, SEQS).astype(jnp.int32)
    fullest = (whole + 1 + jax.random.randint(key_full, (), 0, SEQS - 1).astype(jnp.int32)) % SEQS
    cuts = jnp.where(order == fullest, 4, cuts)
    cuts = jnp.where(order == whole, 0, cuts)
    room = SEQLEN - (cuts + 1) * MIN_DOC
    raw = jax.random.randint(key_cut, (SEQS, 4), 0, room[:, None] + 1).astype(jnp.int32)
    slot = jnp.arange(4, dtype=jnp.int32)[None, :]
    active = slot < cuts[:, None]
    ordered = jnp.sort(jnp.where(active, raw, SEQLEN), axis=1)
    bounds = jnp.where(active, ordered + (slot + 1) * MIN_DOC, SEQLEN)
    place = jnp.arange(SEQLEN, dtype=jnp.int32)
    crossed = (place[None, :, None] >= bounds[:, None, :]).astype(jnp.int32)
    return jnp.sum(crossed, axis=2).astype(jnp.int32)


def draw_m_qkv(key, part):
    key = jax.random.fold_in(key, 11)
    return first_moment(key, (D, QKVD), 2.0)


def draw_m_gu(key, part):
    key = jax.random.fold_in(key, 12)
    return first_moment(key, (D, 2 * FF), 0.5)


def draw_m_o(key, part):
    key = jax.random.fold_in(key, 13)
    return first_moment(key, (QD, D), 0.1)


def draw_m_down(key, part):
    key = jax.random.fold_in(key, 14)
    return first_moment(key, (FF, D), 0.5)


def draw_m_gains(key, part):
    key = jax.random.fold_in(key, 15)
    return first_moment(key, (2 * D + 2 * HD,), 4.0)


def draw_v_qkv(key, part):
    key = jax.random.fold_in(key, 21)
    return second_moment(key, (D, QKVD), 2.0)


def draw_v_gu(key, part):
    key = jax.random.fold_in(key, 22)
    return second_moment(key, (D, 2 * FF), 0.5)


def draw_v_o(key, part):
    key = jax.random.fold_in(key, 23)
    return second_moment(key, (QD, D), 0.1)


def draw_v_down(key, part):
    key = jax.random.fold_in(key, 24)
    return second_moment(key, (FF, D), 0.5)


def draw_v_gains(key, part):
    key = jax.random.fold_in(key, 25)
    return second_moment(key, (2 * D + 2 * HD,), 4.0)


def levels(rng, shape, pieces, low, high):
    factor_of = 1.0
    for position, shards_of in pieces:
        heights = jax.random.uniform(jax.random.fold_in(jax.random.fold_in(rng, 6), position), (shards_of,), jnp.float32, low / len(pieces), high / len(pieces))
        factor_of = factor_of * jnp.repeat(jnp.exp(heights), shape[position] // shards_of).reshape((-1,) + (1,) * (len(shape) - 1 - position))
    return factor_of


def noise(key, dims, scale, reach, pieces=(), kind=jnp.bfloat16):
    level = levels(key, dims, pieces, -0.22, 0.18) if pieces else 1.0
    values = jax.random.normal(key, dims, jnp.float32) * scale * level
    return jnp.minimum(jnp.maximum(values, -reach), reach).astype(kind)


def setup_inputs(seed: int = 0) -> dict:
    key_list = jax.random.split(jax.random.key(seed), 19)
    hidden = noise(key_list[0], (SEQS, SEQLEN, D), 1.0, 6.0, ((0, 8), (1, 16)))
    cotangent = noise(key_list[1], (SEQS, SEQLEN, D), 1.0, 6.0, ((0, 8), (1, 16)))
    segments = draw_segments(jax.random.fold_in(key_list[18], 71), 0)
    w_qkv = noise(key_list[3], (D, QKVD), D ** -0.5, 0.1875, ((0, 16),), jnp.float32)
    w_gu = noise(key_list[4], (D, 2 * FF), D ** -0.5, 0.1875, ((0, 16),), jnp.float32)
    w_o = noise(key_list[5], (QD, D), (QD * 4 // KEYS_SEEN) ** -0.5, 1.5, ((0, 16),), jnp.float32)
    w_down = noise(key_list[6], (FF, D), FF ** -0.5, 0.109375, ((0, 16),), jnp.float32)
    norm_gains = jnp.clip(1.0 + 0.1 * jax.random.normal(key_list[7], (2 * D + 2 * HD,), jnp.float32), 0.5, 1.5)
    m_qkv = draw_m_qkv(jax.random.fold_in(key_list[18], 71), 0)
    m_gu = draw_m_gu(jax.random.fold_in(key_list[18], 71), 0)
    m_o = draw_m_o(jax.random.fold_in(key_list[18], 71), 0)
    m_down = draw_m_down(jax.random.fold_in(key_list[18], 71), 0)
    m_gains = draw_m_gains(jax.random.fold_in(key_list[18], 71), 0)
    v_qkv = draw_v_qkv(jax.random.fold_in(key_list[18], 71), 0)
    v_gu = draw_v_gu(jax.random.fold_in(key_list[18], 71), 0)
    v_o = draw_v_o(jax.random.fold_in(key_list[18], 71), 0)
    v_down = draw_v_down(jax.random.fold_in(key_list[18], 71), 0)
    v_gains = draw_v_gains(jax.random.fold_in(key_list[18], 71), 0)
    return {"hidden": hidden, "cotangent": cotangent, "segments": segments, "w_qkv": w_qkv, "w_gu": w_gu, "w_o": w_o, "w_down": w_down, "norm_gains": norm_gains, "m_qkv": m_qkv, "m_gu": m_gu, "m_o": m_o, "m_down": m_down, "m_gains": m_gains, "v_qkv": v_qkv, "v_gu": v_gu, "v_o": v_o, "v_down": v_down, "v_gains": v_gains}


@jax.custom_vjp
def low(v):
    return lax.optimization_barrier(v.astype(jnp.bfloat16)).astype(jnp.float32)

@jax.custom_vjp
def low_back(v):
    return v

def low_keep(v):
    return (low(v), None)

def low_pass(kept, grad):
    return (grad,)

def back_keep(v):
    return (v, None)

def back_low(kept, grad):
    return (low(grad),)
low.defvjp(low_keep, low_pass)
low_back.defvjp(back_keep, back_low)
EPSILON = 1e-06
THETA = 1000000.0
MASKED = -1e+30
BETA_ONE = 0.9
BETA_TWO = 0.95
ADAM_EPSILON = 1e-08
DECAY = 0.1
STEP_SCALE = 1.5
GAIN_RATE = 0.8

def product(left, right):
    return jnp.dot(left, right, precision=lax.Precision.HIGHEST, preferred_element_type=jnp.float32)

def rms_norm(value, gain):
    return value * lax.rsqrt(lax.optimization_barrier(jnp.mean(value * value, axis=-1, keepdims=True)) + EPSILON) * gain

def turn(value):
    half = value.shape[-1] // 2
    return jnp.concatenate([-value[..., half:], value[..., :half]], axis=-1)

def rope_tables(length):
    positions = jnp.arange(length, dtype=jnp.int32).astype(jnp.float32)
    freq = THETA ** (-jnp.arange(0, HD, 2).astype(jnp.float32) / HD)
    angle = positions[:, None] * freq[None, :]
    angle = jnp.concatenate([angle, angle], axis=-1)
    return (jnp.cos(angle)[:, None, :], jnp.sin(angle)[:, None, :])

def attend(query, keys, values, doc_row):
    length = query.shape[0]
    block = math.gcd(512, length)
    count = length // block
    scale = HD ** (-0.5)
    key_index = jnp.arange(length, dtype=jnp.int32)
    query_blocks = query.reshape(count, block, KVH, H // KVH, HD)
    index_blocks = key_index.reshape(count, block)
    doc_blocks = doc_row.reshape(count, block)

    def one_block(item):
        query_part, index_part, doc_part = item
        score = jnp.einsum('tkgd,skd->kgts', query_part, keys, precision=lax.Precision.HIGHEST) * scale
        score = low_back(score)
        allowed = (doc_part[:, None] == doc_row[None, :]) & (key_index[None, :] <= index_part[:, None])
        score = jnp.where(allowed[None, None], score, MASKED)
        top = lax.optimization_barrier(jnp.max(score, axis=-1, keepdims=True))
        weight = jnp.exp(score - top)
        prob = low(weight / lax.optimization_barrier(jnp.sum(weight, axis=-1, keepdims=True)))
        return jnp.einsum('kgts,skd->tkgd', prob, values, precision=lax.Precision.HIGHEST)
    mixed = lax.map(jax.checkpoint(one_block), (query_blocks, index_blocks, doc_blocks))
    return mixed.reshape(length, H * HD)

def layer(hidden, w_qkv, w_gu, w_o, w_down, norm_gains, doc_row):
    length = hidden.shape[0]
    gain_attn = norm_gains[:D]
    gain_mlp = norm_gains[D:2 * D]
    gain_query = norm_gains[2 * D:2 * D + HD]
    gain_key = norm_gains[2 * D + HD:]
    normed = low(rms_norm(hidden, gain_attn))
    qkv = low_back(product(normed, w_qkv))
    query = qkv[:, :H * HD].reshape(length, H, HD)
    keys = qkv[:, H * HD:(H + KVH) * HD].reshape(length, KVH, HD)
    values = low(qkv[:, (H + KVH) * HD:].reshape(length, KVH, HD))
    cosine, sine = rope_tables(length)
    query = rms_norm(query, gain_query)
    query = low(query * cosine + turn(query) * sine)
    keys = rms_norm(keys, gain_key)
    keys = low(keys * cosine + turn(keys) * sine)
    mixed = attend(query.reshape(length, KVH, H // KVH, HD), keys, values, doc_row)
    mixed = low(low_back(mixed))
    middle = hidden + low_back(product(mixed, w_o))
    normed_two = low(rms_norm(middle, gain_mlp))
    gate_up = low_back(product(normed_two, w_gu))
    inner = low(jax.nn.silu(gate_up[:, :FF]) * gate_up[:, FF:])
    return middle + low_back(product(inner, w_down))

def adam(weight, grad, first, second, rate, decay):
    first = BETA_ONE * first + (1.0 - BETA_ONE) * grad
    second = BETA_TWO * second + (1.0 - BETA_TWO) * grad * grad
    ratio = first / (1.0 - BETA_ONE ** STEP) / (jnp.sqrt(second / (1.0 - BETA_TWO ** STEP)) + ADAM_EPSILON)
    return (first, second, weight - rate * (ratio + decay * weight))

def reference(hidden, cotangent, segments, w_qkv, w_gu, w_o, w_down, norm_gains, m_qkv, m_gu, m_o, m_down, m_gains, v_qkv, v_gu, v_o, v_down, v_gains):
    masters = (w_qkv, w_gu, w_o, w_down, norm_gains)
    rounded = tuple((lax.optimization_barrier(w.astype(jnp.bfloat16)).astype(jnp.float32) for w in masters))

    def per_sequence(totals, item):
        row, grad_row, doc_row = item

        def forward(start, *weights):
            return layer(start, *weights, doc_row)
        result, pullback = jax.vjp(forward, row.astype(jnp.float32), *rounded)
        grads = pullback(grad_row.astype(jnp.float32))
        totals = tuple((total + grad for total, grad in zip(totals, grads[1:])))
        return (totals, (result.astype(jnp.bfloat16), grads[0]))
    zeros = tuple((jnp.zeros(w.shape, jnp.float32) for w in masters))
    totals, (output, hidden_grad) = lax.scan(per_sequence, zeros, (hidden, cotangent, segments))
    rates = (STEP_SCALE / math.sqrt(D), STEP_SCALE / math.sqrt(D), STEP_SCALE / math.sqrt(H * HD * 4 // KEYS_SEEN), STEP_SCALE / math.sqrt(FF), GAIN_RATE)
    decays = (DECAY, DECAY, DECAY, DECAY, 0.0)
    firsts = (m_qkv, m_gu, m_o, m_down, m_gains)
    seconds = (v_qkv, v_gu, v_o, v_down, v_gains)
    updated = []
    for index in range(5):
        updated.extend(adam(masters[index], totals[index], firsts[index], seconds[index], rates[index], decays[index]))
    return (output, hidden_grad, updated[0], updated[1], updated[2], updated[3], updated[4], updated[5], updated[6], updated[7], updated[8], updated[9], updated[10], updated[11], updated[12], updated[13], updated[14])
```

```python
import functools
import math

import jax
import jax.numpy as jnp
import numpy as np
from jax import lax
from jax.experimental import pallas as pl
from jax.experimental.pallas import tpu as pltpu
from jax.sharding import Mesh
from jax.sharding import PartitionSpec as P

D = 1024
H = 16
KVH = 8
HD = 128
FF = 3072
KEYS_SEEN = 512
STEP = 10
SEQLEN = 2048
EPSILON = 1e-06
THETA = 1000000.0
BETA_ONE = 0.9
BETA_TWO = 0.95
ADAM_EPSILON = 1e-08
DECAY = 0.1
STEP_SCALE = 1.5
GAIN_RATE = 0.8

SCALE = HD**-0.5
LOG2E = math.log2(math.e)
FAR = 1024.0
BLK = 512

DP = ("xlo", "z")
SEQ = ("xhi", "y", "core")
CHIPS = ("xhi", "y")
YC = ("y", "core")
BF = jnp.bfloat16
F32 = jnp.float32


def mm(a, b):
    return jnp.dot(a, b, preferred_element_type=F32)


def mm_nt(a, b):
    return lax.dot_general(a, b, (((1,), (1,)), ((), ())), preferred_element_type=F32)


def mm_tn(a, b):
    return lax.dot_general(a, b, (((0,), (0,)), ((), ())), preferred_element_type=F32)


def normalize(value):
    factor = lax.rsqrt(jnp.mean(value * value, axis=-1, keepdims=True) + EPSILON)
    return value * factor, factor


def norm_back(grad_unit, unit, factor):
    return factor * (grad_unit - unit * jnp.mean(grad_unit * unit, axis=-1, keepdims=True))


def rope_tables():
    freq = np.float32(THETA) ** (-np.arange(0, HD, 2).astype(np.float32) / np.float32(HD))
    angle = np.arange(SEQLEN, dtype=np.float32)[:, None] * freq.astype(np.float32)[None, :]
    cosine, sine = np.cos(angle), np.sin(angle)
    return (
        np.concatenate([cosine, cosine], 1).astype(np.float32),
        np.concatenate([-sine, sine], 1).astype(np.float32),
    )


def swap_core(value):
    return lax.ppermute(value, "core", [(0, 1), (1, 0)])


def swap_xhi(value):
    return lax.ppermute(value, "xhi", [(0, 1), (1, 0)])


def all_to_all(value, axes):
    return lax.all_to_all(value, axes, split_axis=0, concat_axis=0, tiled=True)


def spread(value, axes, count):
    return all_to_all(jnp.broadcast_to(value[None], (count, *value.shape)), axes)


def qkv_kernel(core, own, other, w, cos, sin, gains, x_out, q_out, k_out, v_out, raw_out):
    first = core[0] == 0
    a, b = own[0], other[0]
    x = jnp.concatenate([jnp.where(first, a, b), jnp.where(first, b, a)], axis=0)
    x_out[...] = x
    qkv = mm(x, w[...])
    raw_out[...] = qkv[:, : 2 * HD]

    def rotated(part, gain):
        unit, _ = normalize(part)
        value = unit * gain
        return value * cos[...] + pltpu.roll(value, HD // 2, 1) * sin[...]

    q_out[...] = (rotated(qkv[:, :HD], gains[0:1, :]) * (SCALE * LOG2E)).astype(BF)
    k_out[...] = rotated(qkv[:, HD : 2 * HD], gains[1:2, :]).astype(BF)
    v_out[...] = qkv[:, 2 * HD :].astype(BF)


def qkv_call(core, own, other, w, cos, sin, gains):
    rows = 256
    part = pl.BlockSpec((1, 128, D), lambda p, c: (p, 0, 0))
    whole = lambda shape: pl.BlockSpec(shape, lambda p, c: (0, 0))
    tokens = lambda width: pl.BlockSpec((rows, width), lambda p, c: (p, 0))
    return pl.pallas_call(
        qkv_kernel,
        grid_spec=pltpu.PrefetchScalarGridSpec(
            num_scalar_prefetch=1,
            grid=(SEQLEN // rows,),
            in_specs=[part, part, whole((D, 3 * HD)), tokens(HD), tokens(HD), whole((8, HD))],
            out_specs=[tokens(D), tokens(HD), tokens(HD), tokens(HD), tokens(2 * HD)],
        ),
        out_shape=[
            jax.ShapeDtypeStruct((SEQLEN, D), BF),
            jax.ShapeDtypeStruct((SEQLEN, HD), BF),
            jax.ShapeDtypeStruct((SEQLEN, HD), BF),
            jax.ShapeDtypeStruct((SEQLEN, HD), BF),
            jax.ShapeDtypeStruct((SEQLEN, 2 * HD), F32),
        ],
        compiler_params=pltpu.CompilerParams(vmem_limit_bytes=24 * 1024 * 1024),
        name="qkv",
    )(core, own, other, w, cos, sin, gains)


def attend_kernel(q, qx, k, kx, v, out, total):
    ones = jnp.ones((BLK, HD), BF)
    causal = lax.broadcasted_iota(jnp.int32, (BLK, BLK), 1) <= lax.broadcasted_iota(
        jnp.int32, (BLK, BLK), 0
    )
    for i in range(SEQLEN // BLK):
        rows = pl.ds(i * BLK, BLK)
        query = jnp.concatenate([q[rows, :], qx[rows, :]], axis=1)
        acc = None
        for j in range(i + 1):
            cols = pl.ds(j * BLK, BLK)
            key = jnp.concatenate([k[cols, :], kx[cols, :]], axis=1)
            prob = jnp.exp2(mm_nt(query, key))
            if i == j:
                prob = jnp.where(causal, prob, 0.0)
            term = mm(prob.astype(BF), jnp.concatenate([v[cols, :], ones], axis=1))
            acc = term if acc is None else acc + term
        total[rows, :] = acc[:, HD:]
        out[rows, :] = (acc[:, :HD] / acc[:, HD:]).astype(BF)


def attend_call(q, qx, k, kx, v):
    return pl.pallas_call(
        attend_kernel,
        out_shape=[
            jax.ShapeDtypeStruct((SEQLEN, HD), BF),
            jax.ShapeDtypeStruct((SEQLEN, HD), F32),
        ],
        compiler_params=pltpu.CompilerParams(vmem_limit_bytes=32 * 1024 * 1024),
        name="attend",
    )(q, qx, k, kx, v)


def thirds(value):
    high = value.astype(BF).astype(F32)
    middle = (value - high).astype(BF).astype(F32)
    return high, middle, value - high - middle


def attend_back_kernel(
    q, qx, k, kx, v, grad, out, total, raw, cos, sin, gains,
    dq_out, dk_out, dv_out, gain_out, qx_s, gx_s, dq_s,
):
    count = SEQLEN // BLK
    lane = lax.broadcasted_iota(jnp.int32, (BLK, HD), 1)
    ones = jnp.ones((BLK, HD), BF)
    causal = lax.broadcasted_iota(jnp.int32, (BLK, BLK), 0) <= lax.broadcasted_iota(
        jnp.int32, (BLK, BLK), 1
    )

    def placed(parts, start):
        value = jnp.zeros((BLK, HD), F32)
        for n, part in enumerate(parts):
            value = jnp.where(lane == start + n, part, value)
        return value

    for i in range(count):
        rows = pl.ds(i * BLK, BLK)
        level = placed(thirds(jnp.log2(total[rows, :])), 8)
        qx_s[rows, :] = (qx[rows, :].astype(F32) - level).astype(BF)
        delta = jnp.sum(grad[rows, :].astype(F32) * out[rows, :].astype(F32), 1, keepdims=True)
        gx_s[rows, :] = (-placed(thirds(delta), 0)).astype(BF)

    def back(value, part, gain, rows):
        turned = value * cos[rows, :] - pltpu.roll(value, HD // 2, 1) * sin[rows, :]
        unit, factor = normalize(raw[rows, pl.ds(part * HD, HD)])
        return (
            norm_back(turned * gain, unit, factor),
            jnp.sum(turned * unit, axis=0, keepdims=True),
        )

    gain_q = jnp.zeros((1, HD), F32)
    gain_k = jnp.zeros((1, HD), F32)
    for j in range(count):
        cols = pl.ds(j * BLK, BLK)
        key = jnp.concatenate([k[cols, :], kx[cols, :]], axis=1)
        value = jnp.concatenate([v[cols, :], ones], axis=1)
        dk = dv = None
        for i in range(j, count):
            rows = pl.ds(i * BLK, BLK)
            query = jnp.concatenate([q[rows, :], qx_s[rows, :]], axis=1)
            given = jnp.concatenate([grad[rows, :], gx_s[rows, :]], axis=1)
            prob = jnp.exp2(mm_nt(key, query))
            if i == j:
                prob = jnp.where(causal, prob, 0.0)
            score = (prob * mm_nt(value, given)).astype(BF)
            dv_term = mm(prob.astype(BF), grad[rows, :])
            dk_term = mm(score, q[rows, :])
            dq_term = mm_tn(score, k[cols, :])
            dv = dv_term if dv is None else dv + dv_term
            dk = dk_term if dk is None else dk + dk_term
            if j == 0:
                dq_s[rows, :] = dq_term
            else:
                dq_s[rows, :] += dq_term
        dv_out[cols, :] = dv.astype(BF)
        dk, gain = back(dk * (1.0 / LOG2E), 1, gains[1:2, :], cols)
        dk_out[cols, :] = dk.astype(BF)
        gain_k += gain
        dq, gain = back(dq_s[cols, :] * SCALE, 0, gains[0:1, :], cols)
        dq_out[cols, :] = dq.astype(BF)
        gain_q += gain
    gain_out[...] = jnp.concatenate([gain_q, gain_k, jnp.zeros((6, HD), F32)], axis=0)


def attend_back_call(*args):
    tokens = jax.ShapeDtypeStruct((SEQLEN, HD), BF)
    return pl.pallas_call(
        attend_back_kernel,
        out_shape=[tokens, tokens, tokens, jax.ShapeDtypeStruct((8, HD), F32)],
        scratch_shapes=[
            pltpu.VMEM((SEQLEN, HD), BF),
            pltpu.VMEM((SEQLEN, HD), BF),
            pltpu.VMEM((SEQLEN, HD), F32),
        ],
        compiler_params=pltpu.CompilerParams(vmem_limit_bytes=40 * 1024 * 1024),
        name="attend_back",
    )(*args)


def adam(weight, grad, first, second, rate, decay):
    first = BETA_ONE * first + (1.0 - BETA_ONE) * grad
    second = BETA_TWO * second + (1.0 - BETA_TWO) * grad * grad
    ratio = (
        first / (1.0 - BETA_ONE**STEP) / (jnp.sqrt(second / (1.0 - BETA_TWO**STEP)) + ADAM_EPSILON)
    )
    return (first, second, weight - rate * (ratio + decay * weight))


def on_device(
    hidden, cotangent, segments, w_qkv, w_gu, w_o, w_down, norm_gains,
    m_qkv, m_gu, m_o, m_down, m_gains, v_qkv, v_gu, v_o, v_down, v_gains,
):
    core = lax.axis_index("core")
    xhi = lax.axis_index("xhi")
    zero_core = core == 0
    zero_xhi = xhi == 0

    def by_core(own, other):
        return jnp.stack(
            [jnp.where(zero_core, own, other), jnp.where(zero_core, other, own)], axis=1
        )

    def by_xhi(own, other):
        return jnp.concatenate(
            [jnp.where(zero_xhi, own, other), jnp.where(zero_xhi, other, own)], axis=0
        )

    low_qkv, low_gu, low_o, low_down = (w.astype(BF) for w in (w_qkv, w_gu, w_o, w_down))
    full_o = lax.all_gather(low_o, SEQ, axis=0, tiled=True)
    grad_out = cotangent[0]
    grad_half = lax.all_gather(grad_out, YC, axis=0, tiled=True)
    full_qkv = lax.all_gather(low_qkv, SEQ, axis=0, tiled=True)

    x = hidden[0].astype(F32)
    unit_one, factor_one = normalize(x)
    columns = jnp.concatenate(
        [
            low_qkv[:, : H * HD].reshape(64, 8, 256),
            low_qkv[:, H * HD : (H + KVH) * HD].reshape(64, 8, HD),
            low_qkv[:, (H + KVH) * HD :].reshape(64, 8, HD),
        ],
        axis=-1,
    ).transpose(1, 0, 2)
    columns = jnp.concatenate([columns[:, :32], columns[:, 32:]], axis=-1)
    small = jnp.concatenate(
        [
            norm_gains.astype(BF),
            jnp.zeros((112,), BF),
            segments[0].astype(BF),
            jnp.zeros((640,), BF),
        ]
    )
    small = jnp.concatenate([small[None], jnp.zeros((15, D), BF)], axis=0)
    same = jnp.concatenate([unit_one.astype(BF), small], axis=0)
    packet = jnp.concatenate([jnp.broadcast_to(same[None], (8, 144, D)), columns], axis=1)
    own = all_to_all(packet, CHIPS)
    other = swap_core(own)

    small = by_core(own[:, 128], other[:, 128]).reshape(16, D)
    gains = small[:, :144].reshape(2304).astype(F32)
    docs = small[:, 256:384].reshape(SEQLEN).astype(F32)
    gain_attn, gain_mlp = gains[:D], gains[D : 2 * D]
    gain_heads = jnp.concatenate([gains[2 * D :].reshape(2, HD), jnp.zeros((6, HD), F32)], axis=0)
    columns = by_core(own[:, 144:], other[:, 144:])
    columns = jnp.concatenate([columns[..., :512], columns[..., 512:]], axis=2).reshape(D, 512)
    w_query = jnp.where(zero_core, columns[:, :HD], columns[:, HD : 2 * HD])
    w_heads = jnp.concatenate([w_query, columns[:, 2 * HD :]], axis=1)
    w_heads_gain = (w_heads.astype(F32) * gain_attn[:, None]).astype(BF)

    lane = jnp.arange(HD, dtype=F32)[None, :]
    same_doc = (docs[:, None] == lane) & (lane < 8)
    qx = jnp.where(same_doc, -FAR, 0.0).astype(BF)
    kx = jnp.where((lane < 16) & ~same_doc, 1.0, 0.0).astype(BF)
    cos, sin = (jnp.asarray(t) for t in rope_tables())

    unit_all, q, k, v, raw = qkv_call(
        core.reshape(1).astype(jnp.int32), own, other, w_heads_gain, cos, sin, gain_heads
    )
    mixed, total = attend_call(q, qx, k, kx, v)

    gu_cols = low_gu.reshape(64, 2, 2, 8, 192).transpose(3, 0, 1, 2, 4).reshape(8, 64, 768)
    gu_half = all_to_all(gu_cols, YC).reshape(512, 768)
    gu = by_xhi(gu_half, swap_xhi(gu_half))
    gu_gain = (gu.astype(F32) * gain_mlp[:, None]).astype(BF)
    down = by_xhi(low_down, swap_xhi(low_down))

    mixed_mine = all_to_all(mixed.reshape(16, 128, HD), SEQ)
    mixed_mine = mixed_mine.transpose(1, 0, 2).reshape(128, H * HD)
    middle = x + mm(mixed_mine, full_o)
    unit_two, factor_two = normalize(middle)

    own = spread(unit_two.astype(BF), "y", 4)
    tokens = by_core(own, swap_core(own)).reshape(1024, D)

    gate_up = mm(tokens, gu_gain)
    gate, up = gate_up[:, :384], gate_up[:, 384:]
    sigmoid = jax.nn.sigmoid(gate)
    silu = gate * sigmoid
    inner = (silu * up).astype(BF)
    grad_inner = mm_nt(grad_half, down)
    grad_gate = grad_inner * up * sigmoid * (1.0 + gate * (1.0 - sigmoid))
    grad_gate_up = jnp.concatenate([grad_gate, grad_inner * silu], axis=-1).astype(BF)
    part = mm_nt(grad_gate_up, gu_gain).reshape(4, 2, 128, D)
    keep = jnp.where(zero_core, part[:, 0], part[:, 1])
    send = jnp.where(zero_core, part[:, 1], part[:, 0]).astype(BF)
    part = (keep + swap_core(send).astype(F32)).astype(BF)
    grad_unit_two = jnp.sum(all_to_all(part, "y").astype(F32), axis=0)

    out_part = mm(inner, down).astype(BF)
    output = middle + lax.psum_scatter(out_part, YC, scatter_dimension=0, tiled=True).astype(F32)

    sum_gu = mm_tn(tokens, grad_gate_up)
    gain_mlp_grad = jnp.sum(sum_gu * gu.astype(F32), axis=1)
    sum_gu = (sum_gu * gain_mlp[:, None]).astype(BF)
    sum_gu = sum_gu.reshape(16, 8, 8, 768).transpose(1, 0, 2, 3).reshape(8 * 128, 768)
    sum_gu = lax.psum_scatter(sum_gu, DP, scatter_dimension=0, tiled=True)
    sum_down = mm_tn(inner, grad_half).astype(BF)
    sum_down = sum_down.reshape(2, 8, 24, D).transpose(1, 0, 2, 3).reshape(8 * 48, D)
    sum_down = lax.psum_scatter(sum_down, DP, scatter_dimension=0, tiled=True)

    grad_middle = grad_out.astype(F32) + norm_back(grad_unit_two, unit_two, factor_two)
    grad_middle_low = grad_middle.astype(BF)
    grad_middle_all = lax.all_gather(grad_middle_low, SEQ, axis=0, tiled=True)
    grad_mixed = mm_nt(grad_middle_low, full_o).astype(BF)
    grad_mixed = grad_mixed.reshape(128, H, HD).transpose(1, 0, 2)
    grad_mixed = all_to_all(grad_mixed, SEQ).reshape(SEQLEN, HD)

    dq, dk, dv, gain_part = attend_back_call(
        q, qx, k, kx, v, grad_mixed, mixed, total, raw, cos, sin, gain_heads
    )
    keep = jnp.where(zero_core, dk, dv).astype(F32)
    got = swap_core(jnp.where(zero_core, dv, dk))
    grad_heads = jnp.concatenate([dq, (keep + got.astype(F32)).astype(BF)], axis=1)

    mine = all_to_all(grad_heads.reshape(16, 128, 256), SEQ)

    def natural(value):
        rows = value.shape[1]
        pick = lambda block: block.transpose(1, 0, 2).reshape(rows, -1)
        pairs = value[:, :, HD:].reshape(8, 2, rows, HD)
        return jnp.concatenate(
            [pick(value[:, :, :HD]), pick(pairs[:, 0]), pick(pairs[:, 1])], axis=1
        )

    grad_unit_one = mm_nt(natural(mine), full_qkv) * gain_attn
    hidden_grad = grad_middle + norm_back(grad_unit_one, unit_one, factor_one)

    sum_heads = mm_tn(unit_all, grad_heads)
    w_kv = jnp.where(zero_core, w_heads[:, HD : 2 * HD], w_heads[:, 2 * HD :])
    w_mine = jnp.concatenate([w_heads[:, :HD], w_kv], axis=1)
    gain_attn_grad = jnp.sum(sum_heads * w_mine.astype(F32), axis=1)
    sum_heads = (sum_heads * gain_attn[:, None]).astype(BF).reshape(16, 64, 256)
    sum_gains = jnp.concatenate(
        [gain_attn_grad, gain_mlp_grad, gain_part[0], gain_part[1]]
    ).astype(BF)
    sum_gains = jnp.pad(sum_gains.reshape(16, 1, 144), ((0, 0), (0, 7), (0, 112)))
    parts_gu = sum_gu.reshape(16, 8, 3, 256).transpose(0, 2, 1, 3).reshape(16, 24, 256)
    packet = jnp.concatenate([sum_heads, parts_gu, sum_gains], axis=1)
    packet = all_to_all(packet, SEQ)
    rows_qkv = natural(packet[:, :64])
    rows_gu = packet[:, 64:88].astype(F32).reshape(2, 8, 3, 8, 256).sum(axis=0)
    rows_gu = rows_gu.transpose(2, 0, 1, 3).reshape(8, 8, 2, 2, 192)
    rows_gu = rows_gu.transpose(0, 2, 3, 1, 4).reshape(48, D).astype(BF)
    part_gains = packet[:, 88, :144].astype(F32).sum(axis=0).astype(BF)
    sum_down = sum_down.reshape(2, 24, D)
    keep = jnp.where(zero_xhi, sum_down[0], sum_down[1]).astype(F32)
    got = swap_xhi(jnp.where(zero_xhi, sum_down[1], sum_down[0]))
    rows_down = (keep + got.astype(F32)).astype(BF)
    rows_o = mm_tn(mixed, grad_middle_all).astype(BF)

    part_gains = jnp.pad(part_gains[None], ((0, 15), (0, D - 144)))
    packet = jnp.concatenate(
        [
            rows_qkv.reshape(8, 32, D),
            rows_o.reshape(8, 16, D),
            jnp.broadcast_to(part_gains[None], (8, 16, D)),
        ],
        axis=1,
    )
    packet = all_to_all(packet, DP).astype(F32).sum(axis=0)
    grad_gains = packet[48, :144]
    packet = jnp.concatenate([packet[:48].astype(BF), rows_gu, rows_down], axis=0)
    packet = spread(packet, DP, 8)
    owned = (
        packet[:, :32].reshape(64, 4096),
        packet[:, 48:96].reshape(64, 6144),
        packet[:, 32:48].reshape(128, D),
        packet[:, 96:].reshape(192, D),
        grad_gains,
    )
    masters = (w_qkv, w_gu, w_o, w_down, norm_gains)
    rates = (
        STEP_SCALE / math.sqrt(D),
        STEP_SCALE / math.sqrt(D),
        STEP_SCALE / math.sqrt(H * HD * 4 // KEYS_SEEN),
        STEP_SCALE / math.sqrt(FF),
        GAIN_RATE,
    )
    decays = (DECAY, DECAY, DECAY, DECAY, 0.0)
    firsts = (m_qkv, m_gu, m_o, m_down, m_gains)
    seconds = (v_qkv, v_gu, v_o, v_down, v_gains)
    results = [output.astype(BF)[None], hidden_grad[None]]
    for index in range(5):
        results.extend(
            adam(
                masters[index],
                owned[index].astype(F32),
                firsts[index],
                seconds[index],
                rates[index],
                decays[index],
            )
        )
    return tuple(results)


def solution(mesh):
    fine = Mesh(mesh.devices.reshape(2, 4, 2, 4, 2), ("xlo", "z", "xhi", "y", "core"))
    tokens = P(DP, SEQ, None)
    rows = P(SEQ, None)
    return jax.shard_map(
        on_device,
        mesh=fine,
        in_specs=(tokens, tokens, P(DP, SEQ))
        + (rows, rows, rows, rows, P(SEQ)) * 3,
        out_specs=(tokens, tokens) + (rows,) * 12 + (P(SEQ),) * 3,
        check_vma=False,
    )
```

```python
import functools
import math

import jax
import jax.numpy as jnp
import numpy as np
from jax import lax
from jax.experimental import pallas as pl
from jax.experimental.pallas import tpu as pltpu
from jax.sharding import Mesh
from jax.sharding import PartitionSpec as P

D = 1024
H = 16
KVH = 8
HD = 128
FF = 3072
KEYS_SEEN = 512
STEP = 10
SEQLEN = 2048
EPSILON = 1e-06
THETA = 1000000.0
BETA_ONE = 0.9
BETA_TWO = 0.95
ADAM_EPSILON = 1e-08
DECAY = 0.1
STEP_SCALE = 1.5
GAIN_RATE = 0.8

SCALE = HD**-0.5
LOG2E = math.log2(math.e)
FAR = 1024.0
BLK = 512

DP = ("xlo", "z")
SEQ = ("xhi", "y", "core")
CHIPS = ("xhi", "y")
YC = ("y", "core")
ALL = DP + SEQ
MIB = 1024 * 1024
BF = jnp.bfloat16
F32 = jnp.float32


def mm(a, b):
    return jnp.dot(a, b, preferred_element_type=F32)


def mm_nt(a, b):
    return lax.dot_general(a, b, (((1,), (1,)), ((), ())), preferred_element_type=F32)


def mm_tn(a, b):
    return lax.dot_general(a, b, (((0,), (0,)), ((), ())), preferred_element_type=F32)


def normalize(value):
    factor = lax.rsqrt(jnp.mean(value * value, axis=-1, keepdims=True) + EPSILON)
    return value * factor, factor


def norm_back(grad_unit, unit, factor):
    return factor * (grad_unit - unit * jnp.mean(grad_unit * unit, axis=-1, keepdims=True))


def rope_table():
    freq = np.float32(THETA) ** (-np.arange(0, HD, 2).astype(np.float32) / np.float32(HD))
    angle = np.arange(SEQLEN, dtype=np.float32)[:, None] * freq.astype(np.float32)[None, :]
    return np.concatenate([np.cos(angle), np.sin(angle)], 1).astype(np.float32)


def swap_core(value):
    return lax.ppermute(value, "core", [(0, 1), (1, 0)])


def swap_x(value):
    return lax.ppermute(value, ("xlo", "xhi"), [(0, 3), (3, 0), (1, 2), (2, 1)])


def swap_xhi(value):
    return lax.ppermute(value, "xhi", [(0, 1), (1, 0)])


def all_to_all(value, axes):
    return lax.all_to_all(value, axes, split_axis=0, concat_axis=0, tiled=True)


def shift_y(value, by):
    return lax.ppermute(value, "y", [(n, (n + by) % 4) for n in range(4)])


def shift_chips(value, dx, dy):
    pairs = [(4 * a + b, 4 * (a ^ dx) + (b + dy) % 4) for a in range(2) for b in range(4)]
    return lax.ppermute(value, CHIPS, pairs)


def tie(*values):
    return lax.optimization_barrier(values)


def spread(value, axes, count):
    return all_to_all(jnp.broadcast_to(value[None], (count, *value.shape)), axes)


def cost(us):
    return pl.CostEstimate(
        flops=int(us * 1.1e9), bytes_accessed=int(us * 2e6), transcendentals=0
    )


SCALARS = pl.BlockSpec(memory_space=pltpu.SMEM)
WHOLE = pl.BlockSpec(memory_space=pltpu.VMEM)


def gather_weights(place, own, other, gain, w, mine_out, back_out):
    first = place[1] == 0
    columns = jnp.transpose(gain[...])
    for p in range(8):
        for c in range(2):
            block = jnp.where(first == (c == 0), own[p], other[p])
            for half in range(2):
                start = (2 * p + c) * 64 + half * 32
                rows = pl.ds(start, 32)
                at = half * 512
                query = jnp.where(first, block[:, at : at + HD], block[:, at + HD : at + 2 * HD])
                key = block[:, at + 2 * HD : at + 3 * HD]
                value = block[:, at + 3 * HD : at + 4 * HD]
                column = columns[start % 128 : start % 128 + 32, start // 128 : start // 128 + 1]
                heads = jnp.concatenate([query, key, value], axis=1).astype(F32) * column
                w[rows, :] = heads.astype(BF)
                mine = jnp.concatenate([query, jnp.where(first, key, value)], axis=1)
                mine_out[rows, :] = mine
                back_out[rows, :] = (mine.astype(F32) * column).astype(BF)


def document_columns(docs, qx, kx):
    columns = jnp.transpose(docs[...])
    lane = lax.broadcasted_iota(jnp.int32, (128, HD), 1)
    for n in range(16):
        rows = pl.ds(128 * n, 128)
        same = columns[:, n : n + 1] == lane.astype(F32)
        qx[rows, :] = jnp.where(same & (lane < 8), -FAR, 0.0).astype(BF)
        kx[rows, :] = jnp.where(same | (lane >= 16), 0.0, 1.0).astype(BF)


def qkv_kernel(
    place, own, other, own_w, other_w, table, gain, gains, docs,
    x_out, q_out, k_out, v_out, raw_out, out, total, qx, kx, mine_out, back_out, q, k, v, w,
):
    step = pl.program_id(0)
    first = place[1] == 0

    @pl.when(step == 0)
    def _():
        gather_weights(place, own_w, other_w, gain, w, mine_out, back_out)
        document_columns(docs, qx, kx)

    a, b = own[0], other[0]
    x = jnp.concatenate([jnp.where(first, a, b), jnp.where(first, b, a)], axis=0)
    x_out[...] = x
    qkv = mm(x, w[...])
    raw_out[...] = qkv[:, : 2 * HD]
    cos, sin = unpack_table(table[...])
    rows = pl.ds(pl.multiple_of(step * 256, 256), 256)

    def rotated(part, gain):
        unit, _ = normalize(part)
        value = unit * gain
        return value * cos + pltpu.roll(value, HD // 2, 1) * sin

    query = (rotated(qkv[:, :HD], gains[0:1, :]) * (SCALE * LOG2E)).astype(BF)
    key = rotated(qkv[:, HD : 2 * HD], gains[1:2, :]).astype(BF)
    value = qkv[:, 2 * HD :].astype(BF)
    q_out[...] = query
    k_out[...] = key
    v_out[...] = value
    q[rows, :] = query
    k[rows, :] = key
    v[rows, :] = value

    @pl.when(step == SEQLEN // 256 - 1)
    def _():
        attend(q, qx, k, kx, v, out, total)


def attend(q, qx, k, kx, v, out, total):
    ones = jnp.ones((BLK, HD), BF)
    causal = lax.broadcasted_iota(jnp.int32, (BLK, BLK), 1) <= lax.broadcasted_iota(
        jnp.int32, (BLK, BLK), 0
    )
    for i in range(SEQLEN // BLK):
        rows = pl.ds(i * BLK, BLK)
        query = jnp.concatenate([q[rows, :], qx[rows, :]], axis=1)
        acc = None
        for j in range(i + 1):
            cols = pl.ds(j * BLK, BLK)
            key = jnp.concatenate([k[cols, :], kx[cols, :]], axis=1)
            prob = jnp.exp2(mm_nt(query, key))
            if i == j:
                prob = jnp.where(causal, prob, 0.0)
            term = mm(prob.astype(BF), jnp.concatenate([v[cols, :], ones], axis=1))
            acc = term if acc is None else acc + term
        total[rows, :] = acc[:, HD:]
        out[rows, :] = (acc[:, :HD] / acc[:, HD:]).astype(BF)


def unpack_table(table):
    low = lax.broadcasted_iota(jnp.int32, table.shape, 1) < HD // 2
    turned = pltpu.roll(table, HD // 2, 1)
    return jnp.where(low, table, turned), jnp.where(low, -turned, table)


def qkv_call(place, own, other, table, gain, gains, docs):
    rows = 256
    part = pl.BlockSpec((1, 128, D), lambda p, c: (p, 0, 0))
    weights = pl.BlockSpec((8, 32, D), lambda p, c: (0, 4, 0))
    whole = lambda shape: pl.BlockSpec(shape, lambda p, c: (0, 0))
    tokens = lambda width: pl.BlockSpec((rows, width), lambda p, c: (p, 0))
    heads = jax.ShapeDtypeStruct((SEQLEN, HD), BF)
    columns = jax.ShapeDtypeStruct((D, 256), BF)
    return pl.pallas_call(
        qkv_kernel,
        grid_spec=pltpu.PrefetchScalarGridSpec(
            num_scalar_prefetch=1,
            grid=(SEQLEN // rows,),
            in_specs=[part, part, weights, weights, tokens(HD)]
            + [whole((8, HD)), whole((8, HD)), whole((16, HD))],
            out_specs=[tokens(D), tokens(HD), tokens(HD), tokens(HD), tokens(2 * HD)]
            + [whole((SEQLEN, HD))] * 4
            + [whole((D, 256))] * 2,
            scratch_shapes=[pltpu.VMEM((SEQLEN, HD), BF)] * 3 + [pltpu.VMEM((D, 384), BF)],
        ),
        out_shape=[
            jax.ShapeDtypeStruct((SEQLEN, D), BF),
            heads,
            heads,
            heads,
            jax.ShapeDtypeStruct((SEQLEN, 2 * HD), F32),
            heads,
            jax.ShapeDtypeStruct((SEQLEN, HD), F32),
            heads,
            heads,
            columns,
            columns,
        ],
        compiler_params=pltpu.CompilerParams(vmem_limit_bytes=58 * MIB),
        cost_estimate=cost(14),
        name="qkv_attend",
    )(place, own, other, own, other, table, gain, gains, docs)


def thirds(value):
    high = value.astype(BF).astype(F32)
    middle = (value - high).astype(BF).astype(F32)
    return high, middle, value - high - middle


def attend_back_kernel(
    place, q, qx, k, kx, v, out, total, gains, grad, raw_hbm, table_hbm,
    dq_out, keep_out, send_out, gain_out, qx_s, gx_s, dq_s, raw, table, sems,
):
    first = place[1] == 0
    late = [
        pltpu.make_async_copy(a, b, sems.at[n])
        for n, (a, b) in enumerate(((raw_hbm, raw), (table_hbm, table)))
    ]
    for copy in late:
        copy.start()
    count = SEQLEN // BLK
    lane = lax.broadcasted_iota(jnp.int32, (BLK, HD), 1)
    ones = jnp.ones((BLK, HD), BF)
    causal = lax.broadcasted_iota(jnp.int32, (BLK, BLK), 0) <= lax.broadcasted_iota(
        jnp.int32, (BLK, BLK), 1
    )

    def placed(parts, start):
        value = jnp.zeros((BLK, HD), F32)
        for n, part in enumerate(parts):
            value = jnp.where(lane == start + n, part, value)
        return value

    for i in range(count):
        rows = pl.ds(i * BLK, BLK)
        level = placed(thirds(jnp.log2(total[rows, :])), 8)
        qx_s[rows, :] = (qx[rows, :].astype(F32) - level).astype(BF)
        delta = jnp.sum(grad[rows, :].astype(F32) * out[rows, :].astype(F32), 1, keepdims=True)
        gx_s[rows, :] = (-placed(thirds(delta), 0)).astype(BF)

    def back(value, part, gain, rows):
        cos, sin = unpack_table(table[rows, :])
        turned = value * cos - pltpu.roll(value, HD // 2, 1) * sin
        unit, factor = normalize(raw[rows, pl.ds(part * HD, HD)])
        return (
            norm_back(turned * gain, unit, factor),
            jnp.sum(turned * unit, axis=0, keepdims=True),
        )

    gain_q = jnp.zeros((1, HD), F32)
    gain_k = jnp.zeros((1, HD), F32)
    for j in range(count):
        cols = pl.ds(j * BLK, BLK)
        key = jnp.concatenate([k[cols, :], kx[cols, :]], axis=1)
        value = jnp.concatenate([v[cols, :], ones], axis=1)
        dk = dv = None
        for i in range(j, count):
            rows = pl.ds(i * BLK, BLK)
            query = jnp.concatenate([q[rows, :], qx_s[rows, :]], axis=1)
            given = jnp.concatenate([grad[rows, :], gx_s[rows, :]], axis=1)
            prob = jnp.exp2(mm_nt(key, query))
            if i == j:
                prob = jnp.where(causal, prob, 0.0)
            score = (prob * mm_nt(value, given)).astype(BF)
            dv_term = mm(prob.astype(BF), grad[rows, :])
            dk_term = mm(score, q[rows, :])
            dq_term = mm_tn(score, k[cols, :])
            dv = dv_term if dv is None else dv + dv_term
            dk = dk_term if dk is None else dk + dk_term
            if j == 0:
                dq_s[rows, :] = dq_term
            else:
                dq_s[rows, :] += dq_term
        if j == 0:
            for copy in late:
                copy.wait()
        dk, gain = back(dk * (1.0 / LOG2E), 1, gains[1:2, :], cols)
        keep_out[cols, :] = jnp.where(first, dk, dv).astype(BF)
        send_out[cols, :] = jnp.where(first, dv, dk).astype(BF)
        gain_k += gain
        dq, gain = back(dq_s[cols, :] * SCALE, 0, gains[0:1, :], cols)
        dq_out[cols, :] = dq.astype(BF)
        gain_q += gain
    gain_out[...] = jnp.concatenate([gain_q, gain_k, jnp.zeros((6, HD), F32)], axis=0)


def attend_back_call(*args):
    tokens = jax.ShapeDtypeStruct((SEQLEN, HD), BF)
    return pl.pallas_call(
        attend_back_kernel,
        out_shape=[tokens, tokens, tokens, jax.ShapeDtypeStruct((8, HD), F32)],
        in_specs=[SCALARS]
        + [WHOLE] * (len(args) - 3)
        + [pl.BlockSpec(memory_space=pl.ANY)] * 2,
        scratch_shapes=[
            pltpu.VMEM((SEQLEN, HD), BF),
            pltpu.VMEM((SEQLEN, HD), BF),
            pltpu.VMEM((SEQLEN, HD), F32),
            pltpu.VMEM((SEQLEN, 2 * HD), F32),
            pltpu.VMEM((SEQLEN, HD), F32),
            pltpu.SemaphoreType.DMA((2,)),
        ],
        compiler_params=pltpu.CompilerParams(vmem_limit_bytes=58 * MIB),
        cost_estimate=cost(12),
        name="attend_back",
    )(*args)


def columns_kernel(w, out):
    for n in range(8):
        for g in range(4):
            part = w[:, pl.ds(192 * (8 * g + n), 192)].astype(BF)
            out[n // 2, n % 2, :, pl.ds(192 * g, 192)] = part
            out[4 + n // 2, n % 2, :, pl.ds(192 * g, 192)] = part


def columns_call(w):
    return pl.pallas_call(
        columns_kernel,
        out_shape=jax.ShapeDtypeStruct((8, 2, 64, 768), BF),
        compiler_params=pltpu.CompilerParams(vmem_limit_bytes=16 * MIB),
        cost_estimate=cost(1),
        name="columns",
    )(w)


def place_kernel(place, own, other, gain, raw_out, gained_out):
    columns = jnp.transpose(gain[...])
    first = place[1] == 0
    for p in range(8):
        for c in range(2):
            rows = pl.ds((2 * p + c) * 64, 64)
            block = jnp.where(first == (c == 0), own[p], other[p])
            raw_out[rows, :] = block
            column = columns[64 * c : 64 * c + 64, p : p + 1]
            gained_out[rows, :] = (block.astype(F32) * column).astype(BF)


def place_call(place, own, other, gain):
    return pl.pallas_call(
        place_kernel,
        out_shape=[jax.ShapeDtypeStruct((D, 768), BF)] * 2,
        in_specs=[SCALARS, WHOLE, WHOLE, WHOLE],
        compiler_params=pltpu.CompilerParams(vmem_limit_bytes=24 * MIB),
        cost_estimate=cost(1.5),
        name="place",
    )(place, own, other, gain)


def collect_kernel(place, got, w, keep_out, send_out):
    def rows_of(c):
        rows = pl.ds(pl.multiple_of(c * 128, 128), 128)
        left = jnp.concatenate([got[n, rows, :] for n in range(8)], axis=1)
        right = jnp.concatenate([w[quarter, n] for n in range(8) for quarter in range(4)], axis=0)
        return mm(left, right)

    send_out[...] = rows_of(1 - place[1]).astype(BF)
    keep_out[...] = rows_of(place[1])


def collect_call(place, got, w):
    return pl.pallas_call(
        collect_kernel,
        out_shape=[jax.ShapeDtypeStruct((128, D), F32), jax.ShapeDtypeStruct((128, D), BF)],
        in_specs=[SCALARS, WHOLE, WHOLE],
        compiler_params=pltpu.CompilerParams(vmem_limit_bytes=32 * MIB),
        cost_estimate=cost(2),
        name="collect",
    )(place, got, w)


def to_heads_kernel(place, mine, others, w, out):
    core = place[1]
    for c, value in ((core, mine), (1 - core, others)):
        rows = pl.ds(pl.multiple_of(c * 128, 128), 128)
        for n in range(8):
            right = jnp.concatenate([w[quarter, n] for quarter in range(4)], axis=0)
            out[n, rows, :] = mm_nt(value[...], right).astype(BF)


def to_heads_call(*args):
    return pl.pallas_call(
        to_heads_kernel,
        out_shape=jax.ShapeDtypeStruct((8, 256, HD), BF),
        in_specs=[SCALARS] + [WHOLE] * 3,
        compiler_params=pltpu.CompilerParams(vmem_limit_bytes=16 * MIB),
        cost_estimate=cost(2),
        name="to_heads",
    )(*args)


def back_kernel(place, query, keep, got, w, keep_out, send_out):
    first = place[1] == 0
    total = (keep[...].astype(F32) + got[...].astype(F32)).astype(BF)
    part = mm_nt(jnp.concatenate([query[...], total], axis=1), w[...]).astype(BF)
    low, high = part[:128], part[128:]
    keep_out[0] = jnp.where(first, low, high)
    send_out[0] = jnp.where(first, high, low)


def back_call(place, query, keep, got, w):
    tokens = pl.BlockSpec((256, HD), lambda p, c: (p, 0))
    chip = pl.BlockSpec((1, 128, D), lambda p, c: (p, 0, 0))
    return pl.pallas_call(
        back_kernel,
        grid_spec=pltpu.PrefetchScalarGridSpec(
            num_scalar_prefetch=1,
            grid=(8,),
            in_specs=[tokens] * 3 + [pl.BlockSpec((D, 256), lambda p, c: (0, 0))],
            out_specs=[chip, chip],
        ),
        out_shape=[jax.ShapeDtypeStruct((8, 128, D), BF)] * 2,
        compiler_params=pltpu.CompilerParams(vmem_limit_bytes=24 * MIB),
        cost_estimate=cost(3),
        name="back",
    )(place, query, keep, got, w)


def merge_kernel(place, keep, got, gains, gains_got, *outs):
    for dx in range(2):
        xhi = place[0] if dx == 0 else 1 - place[0]
        for dy in range(4):
            chip = 4 * xhi + lax.rem(place[2] + dy, 4)
            out = outs[4 * dx + dy]
            total = keep[chip].astype(F32) + got[chip].astype(F32)
            out[pl.ds(0, 128), :] = total.astype(BF)
            rows = gains[chip].astype(F32) + gains_got[chip].astype(F32)
            row = jnp.where(place[1] == 0, rows[0:1], rows[1:2])
            row = jnp.concatenate([row, jnp.zeros((1, D - 256), F32)], axis=1)
            out[pl.ds(128, 16), :] = jnp.broadcast_to(row, (16, D)).astype(BF)


def merge_call(*args):
    return pl.pallas_call(
        merge_kernel,
        out_shape=[jax.ShapeDtypeStruct((144, D), BF)] * 8,
        in_specs=[SCALARS] + [WHOLE] * 4,
        compiler_params=pltpu.CompilerParams(vmem_limit_bytes=24 * MIB),
        cost_estimate=cost(2),
        name="merge",
    )(*args)


def mlp_kernel(own, other, own_given, other_given, w, part_out, inner_out, grad_out):
    mine = pl.program_id(0) < 2
    x = jnp.where(mine, own[...], other[...])
    given = jnp.where(mine, own_given[...], other_given[...])
    gate_up = mm(x, w[...])
    gate, up = gate_up[:, :384], gate_up[:, 384:]
    sigmoid = jax.nn.sigmoid(gate)
    silu = gate * sigmoid
    inner_out[...] = (silu * up).astype(BF)
    grad_gate = given * up * sigmoid * (1.0 + gate * (1.0 - sigmoid))
    grad = jnp.concatenate([grad_gate, given * silu], axis=1).astype(BF)
    grad_out[...] = grad
    part_out[...] = mm_nt(grad, w[...]).astype(BF)


def mlp_call(own, other, own_given, other_given, w):
    rows = 256
    first = lambda width: pl.BlockSpec((rows, width), lambda i: (jnp.minimum(i, 1), 0))
    second = lambda width: pl.BlockSpec((rows, width), lambda i: (jnp.maximum(i - 2, 0), 0))
    tokens = lambda width: pl.BlockSpec((rows, width), lambda i: (i, 0))
    return pl.pallas_call(
        mlp_kernel,
        grid=(1024 // rows,),
        in_specs=[first(D), second(D), first(384), second(384)]
        + [pl.BlockSpec((D, 768), lambda i: (0, 0))],
        out_specs=[tokens(D), tokens(384), tokens(768)],
        out_shape=[
            jax.ShapeDtypeStruct((1024, D), BF),
            jax.ShapeDtypeStruct((1024, 384), BF),
            jax.ShapeDtypeStruct((1024, 768), BF),
        ],
        compiler_params=pltpu.CompilerParams(vmem_limit_bytes=24 * MIB),
        cost_estimate=cost(6.2),
        name="mlp",
    )(own, other, own_given, other_given, w)


def product_of_parts(xs, ds):
    total, start = None, 0
    for n in range(max(len(xs), len(ds))):
        x, d = xs[min(n, len(xs) - 1)], ds[min(n, len(ds) - 1)]
        rows = min(x.shape[0], d.shape[0])
        x = x[pl.ds(start, rows), :] if x.shape[0] > rows else x[...]
        d = d[pl.ds(start, rows), :] if d.shape[0] > rows else d[...]
        term = mm_tn(x, d)
        total = term if total is None else total + term
        start += rows
    return total


def grad_columns_kernel(counts, *refs):
    a, b = counts
    gain, w, out, gain_out = refs[a + b :]
    total = product_of_parts(refs[:a], refs[a : a + b])
    gain_out[...] = jnp.sum(total * w[...].astype(F32), axis=1, keepdims=True)
    total = total * gain[...]
    for q in range(8):
        for j in range(4):
            piece = total[64 * j + 8 * q : 64 * j + 8 * q + 8]
            groups = [piece[:, g : g + 256] for g in range(0, piece.shape[1], 256)]
            out[q, j] = jnp.concatenate(groups, axis=0).astype(BF)


def grad_columns_call(xs, ds, gain, w):
    width = w.shape[1]
    return pl.pallas_call(
        functools.partial(grad_columns_kernel, (len(xs), len(ds))),
        grid=(4,),
        in_specs=[pl.BlockSpec((x.shape[0], 256), lambda t: (0, t)) for x in xs]
        + [pl.BlockSpec(d.shape, lambda t: (0, 0)) for d in ds]
        + [pl.BlockSpec((256, 1), lambda t: (t, 0)), pl.BlockSpec((256, width), lambda t: (t, 0))],
        out_specs=[
            pl.BlockSpec((8, 4, width // 32, 256), lambda t: (0, t, 0, 0)),
            pl.BlockSpec((256, 1), lambda t: (t, 0)),
        ],
        out_shape=[
            jax.ShapeDtypeStruct((8, 16, width // 32, 256), BF),
            jax.ShapeDtypeStruct((D, 1), F32),
        ],
        compiler_params=pltpu.CompilerParams(vmem_limit_bytes=24 * MIB),
        cost_estimate=cost(3.4),
        name="grad_columns",
    )(*xs, *ds, gain, w)


def rows_kernel(got, out):
    for n in range(8):
        total = got[n].astype(F32) + got[8 + n].astype(F32)
        total = jnp.concatenate([total[0:8], total[8:16], total[16:24]], axis=1)
        for g in range(4):
            out[:, pl.ds(192 * (8 * g + n), 192)] = total[:, 192 * g : 192 * g + 192]


def rows_call(got):
    return pl.pallas_call(
        rows_kernel,
        out_shape=jax.ShapeDtypeStruct((8, 2 * FF), F32),
        compiler_params=pltpu.CompilerParams(vmem_limit_bytes=16 * MIB),
        cost_estimate=cost(1),
        name="rows",
    )(got)


def grad_rows_kernel(counts, *refs):
    a, b = counts
    out = refs[a + b]
    step = out.shape[2] // 2
    total = product_of_parts(refs[:a], refs[a : a + b])
    for q in range(8):
        low, high = q * step, (8 + q) * step
        piece = jnp.concatenate([total[low : low + step], total[high : high + step]], axis=0)
        out[q, 0] = piece.astype(BF)


def grad_rows_call(xs, ds):
    rows = xs[0].shape[1] // 8
    return pl.pallas_call(
        functools.partial(grad_rows_kernel, (len(xs), len(ds))),
        grid=(4,),
        in_specs=[pl.BlockSpec(x.shape, lambda t: (0, 0)) for x in xs]
        + [pl.BlockSpec((d.shape[0], 256), lambda t: (0, t)) for d in ds],
        out_specs=pl.BlockSpec((8, 1, rows, 256), lambda t: (0, t, 0, 0)),
        out_shape=jax.ShapeDtypeStruct((8, 4, rows, 256), BF),
        compiler_params=pltpu.CompilerParams(vmem_limit_bytes=24 * MIB),
        cost_estimate=cost(3),
        name="grad_rows",
    )(*xs, *ds)


def adam(weight, grad, first, second, rate, decay):
    first = BETA_ONE * first + (1.0 - BETA_ONE) * grad
    second = BETA_TWO * second + (1.0 - BETA_TWO) * grad * grad
    ratio = (
        first / (1.0 - BETA_ONE**STEP) / (jnp.sqrt(second / (1.0 - BETA_TWO**STEP)) + ADAM_EPSILON)
    )
    return (first, second, weight - rate * (ratio + decay * weight))


def on_device(
    hidden, cotangent, segments, w_qkv, w_gu, w_o, w_down, norm_gains,
    m_qkv, m_gu, m_o, m_down, m_gains, v_qkv, v_gu, v_o, v_down, v_gains,
):
    core = lax.axis_index("core")
    xhi = lax.axis_index("xhi")
    zero_core = core == 0
    zero_xhi = xhi == 0
    y = lax.axis_index("y")
    z = lax.axis_index("z")
    place = jnp.stack([xhi, core, y]).astype(jnp.int32)

    def by_xhi(own, other, axis=0):
        return jnp.concatenate(
            [jnp.where(zero_xhi, own, other), jnp.where(zero_xhi, other, own)], axis=axis
        )

    def back_by_y(value):
        return jnp.concatenate(
            [lax.dynamic_slice_in_dim(value, (y + 4 - r) % 4, 1, 0) for r in range(4)], axis=0
        )

    grad_out = cotangent[0]
    low_qkv, low_o, low_down = (w.astype(BF) for w in (w_qkv, w_o, w_down))

    x = hidden[0].astype(F32)
    unit_one, factor_one = normalize(x)
    columns = jnp.concatenate(
        [
            low_qkv[:, : H * HD].reshape(64, 8, 256),
            low_qkv[:, H * HD : (H + KVH) * HD].reshape(64, 8, HD),
            low_qkv[:, (H + KVH) * HD :].reshape(64, 8, HD),
        ],
        axis=-1,
    ).transpose(1, 0, 2)
    columns = jnp.concatenate([columns[:, :32], columns[:, 32:]], axis=-1)
    small = jnp.concatenate(
        [
            norm_gains.astype(BF),
            jnp.zeros((112,), BF),
            segments[0].astype(BF),
            jnp.zeros((640,), BF),
        ]
    )
    small = jnp.concatenate([small[None], jnp.zeros((15, D), BF)], axis=0)
    quarter_o = lax.dynamic_slice_in_dim(low_o, z * 32, 32, 0)
    spread_x = jnp.broadcast_to(unit_one.astype(BF)[None], (8, 128, D))
    same = jnp.concatenate([quarter_o, small], axis=0)
    same = jnp.broadcast_to(same[None], (8, 48, D))
    packet = jnp.concatenate([spread_x, columns, same], axis=1)
    own = all_to_all(packet, CHIPS)
    dy_own = lax.all_gather(grad_out, "y", axis=0, tiled=False)
    gu_columns = columns_call(w_gu)
    own, low_down, gu_columns, dy_own = tie(own, low_down, gu_columns, dy_own)
    other = swap_core(own)
    small = jnp.stack(
        [
            jnp.where(zero_core, own[:, 192], other[:, 192]),
            jnp.where(zero_core, other[:, 192], own[:, 192]),
        ],
        axis=1,
    ).reshape(16, D)
    gains = small[:, :144].reshape(2304).astype(F32)
    docs = small[:, 256:384].astype(F32)
    gain_attn, gain_mlp = gains[:D], gains[D : 2 * D]
    gain_attn_column, gain_mlp_column = gain_attn[:, None], gain_mlp[:, None]
    gain_heads = jnp.concatenate([gains[2 * D :].reshape(2, HD), jnp.zeros((6, HD), F32)], axis=0)
    table = jnp.asarray(rope_table())

    gu_columns = all_to_all(gu_columns, CHIPS)
    far_down = swap_x(low_down)

    sides_o = lax.all_gather(own[:, 160:192], "z", axis=0, tiled=False)
    unit_all, q, k, v, raw, mixed, total, qx, kx, w_mine, w_back = qkv_call(
        place, own, other, table, gain_attn.reshape(8, HD), gain_heads, docs
    )
    mixed, gu_columns, far_down, low_down, dy_own = tie(
        mixed, gu_columns, far_down, low_down, dy_own
    )

    got = all_to_all(mixed.reshape(8, 256, HD), CHIPS)

    own_gu = jnp.where(zero_core, gu_columns[:, 0], gu_columns[:, 1])
    other_gu = swap_core(jnp.where(zero_core, gu_columns[:, 1], gu_columns[:, 0]))
    gu, gu_gain = place_call(place, own_gu, other_gu, gain_mlp.reshape(8, HD))
    down = by_xhi(low_down, far_down)
    dy_own = back_by_y(dy_own).reshape(512, D)
    dy_other = swap_core(dy_own)
    inner_grad_own = mm_nt(dy_own, down)
    inner_grad_other = mm_nt(dy_other, down)
    got, gu, gu_gain, inner_grad_own, inner_grad_other = tie(
        got, gu, gu_gain, inner_grad_own, inner_grad_other
    )

    keep, send = collect_call(place, got, sides_o)
    middle = x + keep + swap_core(send).astype(F32)
    unit_two, factor_two = normalize(middle)
    unit_two_low = unit_two.astype(BF)
    tokens_own = jnp.concatenate(
        [unit_two_low] + [shift_y(unit_two_low, r) for r in range(1, 4)], axis=0
    )
    tokens_own, mixed = tie(tokens_own, mixed)
    halves = mixed.reshape(2, 1024, HD)
    mixed_keep = jnp.where(zero_xhi, halves[0], halves[1])
    mixed_send = jnp.where(zero_xhi, halves[1], halves[0])
    tokens_other = swap_core(tokens_own)
    part, inner, grad_gu = mlp_call(
        tokens_own, tokens_other, inner_grad_own, inner_grad_other, gu_gain
    )
    part = (part[:512].astype(F32) + swap_core(part[512:]).astype(F32)).astype(BF)

    part, mixed_send, tokens_own, tokens_other, inner, grad_gu = tie(
        part, mixed_send, tokens_own, tokens_other, inner, grad_gu
    )
    shifted = [shift_y(part[128 * r : 128 * r + 128], -r) for r in range(1, 4)]
    sum_gu, gain_mlp_grad = grad_columns_call(
        (tokens_own, tokens_other), (grad_gu,), gain_mlp_column, gu
    )
    sum_down = grad_rows_call((inner,), (dy_own, dy_other))
    packet = jnp.concatenate([sum_gu.reshape(8, 384, 256), sum_down.reshape(8, 192, 256)], axis=1)
    out_part = mm(inner[:512], down) + swap_core(mm(inner[512:], down).astype(BF)).astype(F32)
    out_part = out_part.astype(BF)
    *shifted, packet, out_part, mixed_got = tie(
        *shifted, packet, out_part, swap_xhi(mixed_send)
    )
    mixed_pair = by_xhi(mixed_keep, mixed_got, axis=1)
    packet = lax.psum_scatter(packet.reshape(8 * 576, 256), DP, scatter_dimension=0, tiled=True)
    grad_unit_two = part[:128].astype(F32)
    for value in shifted:
        grad_unit_two += value.astype(F32)
    grad_middle = grad_out.astype(F32) + norm_back(grad_unit_two, unit_two, factor_two)
    grad_middle_low = grad_middle.astype(BF)
    grad_middle_half = lax.all_gather(grad_middle_low, YC, axis=0, tiled=True)
    blocks = to_heads_call(place, grad_middle_low, swap_core(grad_middle_low), sides_o)
    blocks, out_part = tie(blocks, out_part)
    grad_mixed = all_to_all(blocks, CHIPS).reshape(SEQLEN, HD)
    out_shifted = [shift_y(out_part[128 * r : 128 * r + 128], -r) for r in range(1, 4)]
    grad_mixed, *out_shifted = tie(grad_mixed, *out_shifted)
    output = middle + out_part[:128].astype(F32)
    for value in out_shifted:
        output += value.astype(F32)

    dq, keep, send, gain_part = attend_back_call(
        place, q, qx, k, kx, v, mixed, total, gain_heads, grad_mixed, raw, table
    )
    dq, keep, send, packet = tie(dq, keep, send, packet)
    parts_gu = all_to_all(packet[:384].reshape(16, 24, 256), SEQ)
    got = swap_core(send)
    mine, theirs = back_call(place, dq, keep, got, w_back)
    dq, keep, got, theirs, parts_gu = tie(dq, keep, got, theirs, parts_gu)
    theirs = swap_core(theirs)

    grad_heads = jnp.concatenate(
        [dq, (keep.astype(F32) + got.astype(F32)).astype(BF)], axis=1
    )
    sum_heads, gain_attn_grad = grad_columns_call(
        (unit_all,), (grad_heads,), gain_attn_column, w_mine
    )
    sum_gains = jnp.concatenate(
        [gain_attn_grad[:, 0], gain_mlp_grad[:, 0], gain_part[0], gain_part[1]]
    ).astype(BF)
    sum_gains = jnp.pad(sum_gains.reshape(8, 2, 144), ((0, 0), (0, 14), (0, 112)))
    blocks = merge_call(place, mine, theirs, sum_gains, swap_core(sum_gains))
    rows_down = packet[384:].reshape(4, 2, 24, 256)
    sum_heads, rows_down, parts_gu, mixed_pair, *blocks = tie(
        sum_heads, rows_down, parts_gu, mixed_pair, *blocks
    )
    sum_heads = all_to_all(sum_heads.reshape(128, 8, 256), ALL)
    blocks = [blocks[0]] + [shift_chips(blocks[n], n // 4, n % 4) for n in range(1, 8)]
    sum_o = grad_rows_call((mixed_pair,), (grad_middle_half,))
    rows_gu = rows_call(parts_gu)
    kept = jnp.where(zero_xhi, rows_down[:, 0], rows_down[:, 1]).astype(F32)
    came = swap_xhi(jnp.where(zero_xhi, rows_down[:, 1], rows_down[:, 0])).astype(F32)
    rows_down = (kept + came).transpose(1, 0, 2).reshape(24, D)
    wide = jnp.concatenate([rows_gu, rows_down.reshape(8, 3 * D)], axis=1).astype(BF)
    sum_heads, sum_o, wide, blocks[1], blocks[2], blocks[3] = tie(
        sum_heads, sum_o, wide, blocks[1], blocks[2], blocks[3]
    )

    rows_o, *blocks = tie(all_to_all(sum_o.reshape(8, 128, 256), DP), *blocks)
    total_back = blocks[0].astype(F32)
    for value in blocks[1:]:
        total_back += value.astype(F32)
    rows_o = rows_o.astype(F32).sum(axis=0).astype(BF).reshape(4, 2, 16, 256)
    kept = jnp.where(zero_xhi, rows_o[:, 0], rows_o[:, 1]).astype(F32)
    came = swap_xhi(jnp.where(zero_xhi, rows_o[:, 1], rows_o[:, 0])).astype(F32)
    rows_o = (kept + came).transpose(1, 0, 2).reshape(16, D).astype(BF)

    parts = sum_heads.reshape(8, 16, 8, 256).astype(F32).sum(axis=0).astype(BF)
    pick = lambda block: block.transpose(1, 0, 2).reshape(8, -1)
    pairs = parts[:, :, HD:].reshape(8, 2, 8, HD)
    rows_qkv = jnp.concatenate(
        [pick(parts[:, :, :HD]), pick(pairs[:, 0]), pick(pairs[:, 1])], axis=1
    )

    wide = lax.all_gather(wide, DP, axis=0, tiled=True)
    rows_o, wide, total_back = tie(rows_o, wide, total_back)
    owned_gu = wide[:, : 2 * FF]
    owned_down = wide[:, 2 * FF :].reshape(192, D)
    hidden_grad = grad_middle + norm_back(total_back[:128], unit_one, factor_one)
    last = jnp.concatenate(
        [rows_qkv.reshape(8, 4, D).transpose(1, 0, 2).reshape(32, D), rows_o]
        + [total_back[128:].astype(BF)],
        axis=0,
    )
    last = spread(last, DP, 8)
    owned_qkv = last[:, :32].reshape(8, 4, 8, D).transpose(0, 2, 1, 3).reshape(64, 4096)
    owned_o = last[:, 32:48].reshape(128, D)
    grad_gains = last[:, 48, :144].astype(F32).sum(axis=0)
    owned = (owned_qkv, owned_gu, owned_o, owned_down, grad_gains)
    masters = (w_qkv, w_gu, w_o, w_down, norm_gains)
    rates = (
        STEP_SCALE / math.sqrt(D),
        STEP_SCALE / math.sqrt(D),
        STEP_SCALE / math.sqrt(H * HD * 4 // KEYS_SEEN),
        STEP_SCALE / math.sqrt(FF),
        GAIN_RATE,
    )
    decays = (DECAY, DECAY, DECAY, DECAY, 0.0)
    firsts = (m_qkv, m_gu, m_o, m_down, m_gains)
    seconds = (v_qkv, v_gu, v_o, v_down, v_gains)
    results = [output.astype(BF)[None], hidden_grad[None]]
    for index in range(5):
        results.extend(
            adam(
                masters[index],
                owned[index].astype(F32),
                firsts[index],
                seconds[index],
                rates[index],
                decays[index],
            )
        )
    return tuple(results)


def solution(mesh):
    fine = Mesh(mesh.devices.reshape(2, 4, 2, 4, 2), ("xlo", "z", "xhi", "y", "core"))
    tokens = P(DP, SEQ, None)
    rows = P(SEQ, None)
    return jax.shard_map(
        on_device,
        mesh=fine,
        in_specs=(tokens, tokens, P(DP, SEQ))
        + (rows, rows, rows, rows, P(SEQ)) * 3,
        out_specs=(tokens, tokens) + (rows,) * 12 + (P(SEQ),) * 3,
        check_vma=False,
    )
```

```python
import functools
import math

import jax
import jax.numpy as jnp
import numpy as np
from jax import lax
from jax.experimental import pallas as pl
from jax.experimental.pallas import tpu as pltpu
from jax.sharding import Mesh
from jax.sharding import PartitionSpec as P

D = 1024
H = 16
KVH = 8
HD = 128
FF = 3072
KEYS_SEEN = 512
STEP = 10
SEQLEN = 2048
EPSILON = 1e-06
THETA = 1000000.0
BETA_ONE = 0.9
BETA_TWO = 0.95
ADAM_EPSILON = 1e-08
DECAY = 0.1
STEP_SCALE = 1.5
GAIN_RATE = 0.8

SCALE = HD**-0.5
LOG2E = math.log2(math.e)
FAR = 1024.0
BLK = 512

DP = ("xlo", "z")
SEQ = ("xhi", "y", "core")
CHIPS = ("xhi", "y")
YC = ("y", "core")
ALL = DP + SEQ
MIB = 1024 * 1024
BF = jnp.bfloat16
F32 = jnp.float32


def mm(a, b):
    return jnp.dot(a, b, preferred_element_type=F32)


def mm_nt(a, b):
    return lax.dot_general(a, b, (((1,), (1,)), ((), ())), preferred_element_type=F32)


def mm_tn(a, b):
    return lax.dot_general(a, b, (((0,), (0,)), ((), ())), preferred_element_type=F32)


def normalize(value):
    factor = lax.rsqrt(jnp.mean(value * value, axis=-1, keepdims=True) + EPSILON)
    return value * factor, factor


def norm_back(grad_unit, unit, factor):
    return factor * (grad_unit - unit * jnp.mean(grad_unit * unit, axis=-1, keepdims=True))


def rope_table():
    freq = np.float32(THETA) ** (-np.arange(0, HD, 2).astype(np.float32) / np.float32(HD))
    angle = np.arange(SEQLEN, dtype=np.float32)[:, None] * freq.astype(np.float32)[None, :]
    return np.concatenate([np.cos(angle), np.sin(angle)], 1).astype(np.float32)


def swap_core(value):
    return lax.ppermute(value, "core", [(0, 1), (1, 0)])


def swap_x(value):
    return lax.ppermute(value, ("xlo", "xhi"), [(0, 3), (3, 0), (1, 2), (2, 1)])


def swap_xhi(value):
    return lax.ppermute(value, "xhi", [(0, 1), (1, 0)])


def all_to_all(value, axes):
    return lax.all_to_all(value, axes, split_axis=0, concat_axis=0, tiled=True)


def shift_y(value, by):
    return lax.ppermute(value, "y", [(n, (n + by) % 4) for n in range(4)])


def shift_chips(value, dx, dy):
    pairs = [(4 * a + b, 4 * (a ^ dx) + (b + dy) % 4) for a in range(2) for b in range(4)]
    return lax.ppermute(value, CHIPS, pairs)


def tie(*values):
    return lax.optimization_barrier(values)


def spread(value, axes, count):
    return all_to_all(jnp.broadcast_to(value[None], (count, *value.shape)), axes)


def cost(us):
    return pl.CostEstimate(
        flops=int(us * 1.1e9), bytes_accessed=int(us * 2e6), transcendentals=0
    )


SCALARS = pl.BlockSpec(memory_space=pltpu.SMEM)
WHOLE = pl.BlockSpec(memory_space=pltpu.VMEM)


def gather_weights(place, own, other, gain, w, mine_out, back_out):
    first = place[1] == 0
    columns = jnp.transpose(gain[...])
    for p in range(8):
        for c in range(2):
            block = jnp.where(first == (c == 0), own[p], other[p])
            for half in range(2):
                start = (2 * p + c) * 64 + half * 32
                rows = pl.ds(start, 32)
                at = half * 512
                query = jnp.where(first, block[:, at : at + HD], block[:, at + HD : at + 2 * HD])
                key = block[:, at + 2 * HD : at + 3 * HD]
                value = block[:, at + 3 * HD : at + 4 * HD]
                column = columns[start % 128 : start % 128 + 32, start // 128 : start // 128 + 1]
                heads = jnp.concatenate([query, key, value], axis=1).astype(F32) * column
                w[rows, :] = heads.astype(BF)
                mine = jnp.concatenate([query, jnp.where(first, key, value)], axis=1)
                mine_out[rows, :] = mine
                back_out[rows, :] = (mine.astype(F32) * column).astype(BF)


def document_columns(docs, qx, kx):
    columns = jnp.transpose(docs[...])
    lane = lax.broadcasted_iota(jnp.int32, (128, HD), 1)
    for n in range(16):
        rows = pl.ds(128 * n, 128)
        same = columns[:, n : n + 1] == lane.astype(F32)
        qx[rows, :] = jnp.where(same & (lane < 8), -FAR, 0.0).astype(BF)
        kx[rows, :] = jnp.where(same | (lane >= 16), 0.0, 1.0).astype(BF)


def qkv_kernel(
    place, own, other, own_w, other_w, table, gain, gains, docs,
    x_out, q_out, k_out, v_out, raw_out, out, total, qx, kx, mine_out, back_out, q, k, v, w,
):
    step = pl.program_id(0)
    first = place[1] == 0

    @pl.when(step == 0)
    def _():
        gather_weights(place, own_w, other_w, gain, w, mine_out, back_out)
        document_columns(docs, qx, kx)

    a, b = own[0], other[0]
    x = jnp.concatenate([jnp.where(first, a, b), jnp.where(first, b, a)], axis=0)
    x_out[...] = x
    qkv = mm(x, w[...])
    raw_out[...] = qkv[:, : 2 * HD]
    cos, sin = unpack_table(table[...])
    rows = pl.ds(pl.multiple_of(step * 256, 256), 256)

    def rotated(part, gain):
        unit, _ = normalize(part)
        value = unit * gain
        return value * cos + pltpu.roll(value, HD // 2, 1) * sin

    query = (rotated(qkv[:, :HD], gains[0:1, :]) * (SCALE * LOG2E)).astype(BF)
    key = rotated(qkv[:, HD : 2 * HD], gains[1:2, :]).astype(BF)
    value = qkv[:, 2 * HD :].astype(BF)
    q_out[...] = query
    k_out[...] = key
    v_out[...] = value
    q[rows, :] = query
    k[rows, :] = key
    v[rows, :] = value

    @pl.when(step == SEQLEN // 256 - 1)
    def _():
        attend(q, qx, k, kx, v, out, total)


def attend(q, qx, k, kx, v, out, total):
    ones = jnp.ones((BLK, HD), BF)
    causal = lax.broadcasted_iota(jnp.int32, (BLK, BLK), 1) <= lax.broadcasted_iota(
        jnp.int32, (BLK, BLK), 0
    )
    for i in range(SEQLEN // BLK):
        rows = pl.ds(i * BLK, BLK)
        query = jnp.concatenate([q[rows, :], qx[rows, :]], axis=1)
        acc = None
        for j in range(i + 1):
            cols = pl.ds(j * BLK, BLK)
            key = jnp.concatenate([k[cols, :], kx[cols, :]], axis=1)
            prob = jnp.exp2(mm_nt(query, key))
            if i == j:
                prob = jnp.where(causal, prob, 0.0)
            term = mm(prob.astype(BF), jnp.concatenate([v[cols, :], ones], axis=1))
            acc = term if acc is None else acc + term
        total[rows, :] = acc[:, HD:]
        out[rows, :] = (acc[:, :HD] / acc[:, HD:]).astype(BF)


def unpack_table(table):
    low = lax.broadcasted_iota(jnp.int32, table.shape, 1) < HD // 2
    turned = pltpu.roll(table, HD // 2, 1)
    return jnp.where(low, table, turned), jnp.where(low, -turned, table)


def qkv_call(place, own, other, table, gain, gains, docs):
    rows = 256
    part = pl.BlockSpec((1, 128, D), lambda p, c: (p, 0, 0))
    weights = pl.BlockSpec((8, 32, D), lambda p, c: (0, 4, 0))
    whole = lambda shape: pl.BlockSpec(shape, lambda p, c: (0, 0))
    tokens = lambda width: pl.BlockSpec((rows, width), lambda p, c: (p, 0))
    heads = jax.ShapeDtypeStruct((SEQLEN, HD), BF)
    columns = jax.ShapeDtypeStruct((D, 256), BF)
    return pl.pallas_call(
        qkv_kernel,
        grid_spec=pltpu.PrefetchScalarGridSpec(
            num_scalar_prefetch=1,
            grid=(SEQLEN // rows,),
            in_specs=[part, part, weights, weights, tokens(HD)]
            + [whole((8, HD)), whole((8, HD)), whole((16, HD))],
            out_specs=[tokens(D), tokens(HD), tokens(HD), tokens(HD), tokens(2 * HD)]
            + [whole((SEQLEN, HD))] * 4
            + [whole((D, 256))] * 2,
            scratch_shapes=[pltpu.VMEM((SEQLEN, HD), BF)] * 3 + [pltpu.VMEM((D, 384), BF)],
        ),
        out_shape=[
            jax.ShapeDtypeStruct((SEQLEN, D), BF),
            heads,
            heads,
            heads,
            jax.ShapeDtypeStruct((SEQLEN, 2 * HD), F32),
            heads,
            jax.ShapeDtypeStruct((SEQLEN, HD), F32),
            heads,
            heads,
            columns,
            columns,
        ],
        compiler_params=pltpu.CompilerParams(vmem_limit_bytes=58 * MIB),
        cost_estimate=cost(14),
        name="qkv_attend",
    )(place, own, other, own, other, table, gain, gains, docs)


def thirds(value):
    high = value.astype(BF).astype(F32)
    middle = (value - high).astype(BF).astype(F32)
    return high, middle, value - high - middle


def attend_back_kernel(
    place, q, qx, k, kx, v, out, total, gains, grad, raw_hbm, table_hbm,
    dq_out, keep_out, send_out, gain_out, qx_s, gx_s, dq_s, raw, table, sems,
):
    first = place[1] == 0
    late = [
        pltpu.make_async_copy(a, b, sems.at[n])
        for n, (a, b) in enumerate(((raw_hbm, raw), (table_hbm, table)))
    ]
    for copy in late:
        copy.start()
    count = SEQLEN // BLK
    lane = lax.broadcasted_iota(jnp.int32, (BLK, HD), 1)
    ones = jnp.ones((BLK, HD), BF)
    causal = lax.broadcasted_iota(jnp.int32, (BLK, BLK), 0) <= lax.broadcasted_iota(
        jnp.int32, (BLK, BLK), 1
    )

    def placed(parts, start):
        value = jnp.zeros((BLK, HD), F32)
        for n, part in enumerate(parts):
            value = jnp.where(lane == start + n, part, value)
        return value

    for i in range(count):
        rows = pl.ds(i * BLK, BLK)
        level = placed(thirds(jnp.log2(total[rows, :])), 8)
        qx_s[rows, :] = (qx[rows, :].astype(F32) - level).astype(BF)
        delta = jnp.sum(grad[rows, :].astype(F32) * out[rows, :].astype(F32), 1, keepdims=True)
        gx_s[rows, :] = (-placed(thirds(delta), 0)).astype(BF)

    def back(value, part, gain, rows):
        cos, sin = unpack_table(table[rows, :])
        turned = value * cos - pltpu.roll(value, HD // 2, 1) * sin
        unit, factor = normalize(raw[rows, pl.ds(part * HD, HD)])
        return (
            norm_back(turned * gain, unit, factor),
            jnp.sum(turned * unit, axis=0, keepdims=True),
        )

    gain_q = jnp.zeros((1, HD), F32)
    gain_k = jnp.zeros((1, HD), F32)
    for j in range(count):
        cols = pl.ds(j * BLK, BLK)
        key = jnp.concatenate([k[cols, :], kx[cols, :]], axis=1)
        value = jnp.concatenate([v[cols, :], ones], axis=1)
        dk = dv = None
        for i in range(j, count):
            rows = pl.ds(i * BLK, BLK)
            query = jnp.concatenate([q[rows, :], qx_s[rows, :]], axis=1)
            given = jnp.concatenate([grad[rows, :], gx_s[rows, :]], axis=1)
            prob = jnp.exp2(mm_nt(key, query))
            if i == j:
                prob = jnp.where(causal, prob, 0.0)
            score = (prob * mm_nt(value, given)).astype(BF)
            dv_term = mm(prob.astype(BF), grad[rows, :])
            dk_term = mm(score, q[rows, :])
            dq_term = mm_tn(score, k[cols, :])
            dv = dv_term if dv is None else dv + dv_term
            dk = dk_term if dk is None else dk + dk_term
            if j == 0:
                dq_s[rows, :] = dq_term
            else:
                dq_s[rows, :] += dq_term
        if j == 0:
            for copy in late:
                copy.wait()
        dk, gain = back(dk * (1.0 / LOG2E), 1, gains[1:2, :], cols)
        keep_out[cols, :] = jnp.where(first, dk, dv).astype(BF)
        send_out[cols, :] = jnp.where(first, dv, dk).astype(BF)
        gain_k += gain
        dq, gain = back(dq_s[cols, :] * SCALE, 0, gains[0:1, :], cols)
        dq_out[cols, :] = dq.astype(BF)
        gain_q += gain
    gain_out[...] = jnp.concatenate([gain_q, gain_k, jnp.zeros((6, HD), F32)], axis=0)


def attend_back_call(*args):
    tokens = jax.ShapeDtypeStruct((SEQLEN, HD), BF)
    return pl.pallas_call(
        attend_back_kernel,
        out_shape=[tokens, tokens, tokens, jax.ShapeDtypeStruct((8, HD), F32)],
        in_specs=[SCALARS]
        + [WHOLE] * (len(args) - 3)
        + [pl.BlockSpec(memory_space=pl.ANY)] * 2,
        scratch_shapes=[
            pltpu.VMEM((SEQLEN, HD), BF),
            pltpu.VMEM((SEQLEN, HD), BF),
            pltpu.VMEM((SEQLEN, HD), F32),
            pltpu.VMEM((SEQLEN, 2 * HD), F32),
            pltpu.VMEM((SEQLEN, HD), F32),
            pltpu.SemaphoreType.DMA((2,)),
        ],
        compiler_params=pltpu.CompilerParams(vmem_limit_bytes=58 * MIB),
        cost_estimate=cost(12),
        name="attend_back",
    )(*args)


def columns_kernel(w, out):
    for n in range(8):
        for g in range(4):
            part = w[:, pl.ds(192 * (8 * g + n), 192)].astype(BF)
            out[n // 2, n % 2, :, pl.ds(192 * g, 192)] = part
            out[4 + n // 2, n % 2, :, pl.ds(192 * g, 192)] = part


def columns_call(w):
    return pl.pallas_call(
        columns_kernel,
        out_shape=jax.ShapeDtypeStruct((8, 2, 64, 768), BF),
        compiler_params=pltpu.CompilerParams(vmem_limit_bytes=16 * MIB),
        cost_estimate=cost(1),
        name="columns",
    )(w)


def place_kernel(place, own, other, gain, raw_out, gained_out):
    columns = jnp.transpose(gain[...])
    first = place[1] == 0
    for p in range(8):
        for c in range(2):
            rows = pl.ds((2 * p + c) * 64, 64)
            block = jnp.where(first == (c == 0), own[p], other[p])
            raw_out[rows, :] = block
            column = columns[64 * c : 64 * c + 64, p : p + 1]
            gained_out[rows, :] = (block.astype(F32) * column).astype(BF)


def place_call(place, own, other, gain):
    return pl.pallas_call(
        place_kernel,
        out_shape=[jax.ShapeDtypeStruct((D, 768), BF)] * 2,
        in_specs=[SCALARS, WHOLE, WHOLE, WHOLE],
        compiler_params=pltpu.CompilerParams(vmem_limit_bytes=24 * MIB),
        cost_estimate=cost(1.5),
        name="place",
    )(place, own, other, gain)


def collect_kernel(place, got, w, keep_out, send_out):
    def rows_of(c):
        rows = pl.ds(pl.multiple_of(c * 128, 128), 128)
        left = jnp.concatenate([got[n, rows, :] for n in range(8)], axis=1)
        right = jnp.concatenate([w[quarter, n] for n in range(8) for quarter in range(4)], axis=0)
        return mm(left, right)

    send_out[...] = rows_of(1 - place[1]).astype(BF)
    keep_out[...] = rows_of(place[1])


def collect_call(place, got, w):
    return pl.pallas_call(
        collect_kernel,
        out_shape=[jax.ShapeDtypeStruct((128, D), F32), jax.ShapeDtypeStruct((128, D), BF)],
        in_specs=[SCALARS, WHOLE, WHOLE],
        compiler_params=pltpu.CompilerParams(vmem_limit_bytes=32 * MIB),
        cost_estimate=cost(2),
        name="collect",
    )(place, got, w)


def to_heads_kernel(place, mine, others, w, out):
    core = place[1]
    for c, value in ((core, mine), (1 - core, others)):
        rows = pl.ds(pl.multiple_of(c * 128, 128), 128)
        for n in range(8):
            right = jnp.concatenate([w[quarter, n] for quarter in range(4)], axis=0)
            out[n, rows, :] = mm_nt(value[...], right).astype(BF)


def to_heads_call(*args):
    return pl.pallas_call(
        to_heads_kernel,
        out_shape=jax.ShapeDtypeStruct((8, 256, HD), BF),
        in_specs=[SCALARS] + [WHOLE] * 3,
        compiler_params=pltpu.CompilerParams(vmem_limit_bytes=16 * MIB),
        cost_estimate=cost(2),
        name="to_heads",
    )(*args)


def join_kernel(place, query, keep, got, near_out, far_out):
    for side, out in ((place[0], near_out), (1 - place[0], far_out)):
        rows = pl.ds(pl.multiple_of(side * 1024, 1024), 1024)
        total = keep[rows, :].astype(F32) + got[rows, :].astype(F32)
        out[...] = jnp.concatenate([query[rows, :], total.astype(BF)], axis=1)


def join_call(*args):
    half = jax.ShapeDtypeStruct((1024, 256), BF)
    return pl.pallas_call(
        join_kernel,
        out_shape=[half, half],
        in_specs=[SCALARS] + [WHOLE] * 3,
        compiler_params=pltpu.CompilerParams(vmem_limit_bytes=24 * MIB),
        cost_estimate=cost(1.5),
        name="join",
    )(*args)


def back_kernel(place, near, far, w_near, w_far, keep_out, send_out):
    first = place[1] == 0
    part = mm_nt(near[...], w_near[...]) + mm_nt(far[...], w_far[...])
    part = part.astype(BF)
    keep_out[0] = jnp.where(first, part[:128], part[128:])
    send_out[0] = jnp.where(first, part[128:], part[:128])


def back_call(place, near, far, w_near, w_far):
    tokens = pl.BlockSpec((256, 256), lambda p, c: (p, 0))
    whole = pl.BlockSpec((D, 256), lambda p, c: (0, 0))
    chip = pl.BlockSpec((1, 128, D), lambda p, c: (p, 0, 0))
    return pl.pallas_call(
        back_kernel,
        grid_spec=pltpu.PrefetchScalarGridSpec(
            num_scalar_prefetch=1,
            grid=(4,),
            in_specs=[tokens, tokens, whole, whole],
            out_specs=[chip, chip],
        ),
        out_shape=[jax.ShapeDtypeStruct((4, 128, D), BF)] * 2,
        compiler_params=pltpu.CompilerParams(vmem_limit_bytes=24 * MIB),
        cost_estimate=cost(3),
        name="back",
    )(place, near, far, w_near, w_far)


def merge_kernel(place, keep, got, *outs):
    for dy in range(4):
        n = lax.rem(place[2] + dy, 4)
        outs[dy][...] = (keep[n].astype(F32) + got[n].astype(F32)).astype(BF)


def merge_call(*args):
    return pl.pallas_call(
        merge_kernel,
        out_shape=[jax.ShapeDtypeStruct((128, D), BF)] * 4,
        in_specs=[SCALARS] + [WHOLE] * 2,
        compiler_params=pltpu.CompilerParams(vmem_limit_bytes=24 * MIB),
        cost_estimate=cost(1),
        name="merge",
    )(*args)


def mlp_kernel(own, other, own_given, other_given, w, part_out, inner_out, grad_out):
    mine = pl.program_id(0) < 2
    x = jnp.where(mine, own[...], other[...])
    given = jnp.where(mine, own_given[...], other_given[...])
    gate_up = mm(x, w[...])
    gate, up = gate_up[:, :384], gate_up[:, 384:]
    sigmoid = jax.nn.sigmoid(gate)
    silu = gate * sigmoid
    inner_out[...] = (silu * up).astype(BF)
    grad_gate = given * up * sigmoid * (1.0 + gate * (1.0 - sigmoid))
    grad = jnp.concatenate([grad_gate, given * silu], axis=1).astype(BF)
    grad_out[...] = grad
    part_out[...] = mm_nt(grad, w[...]).astype(BF)


def mlp_call(own, other, own_given, other_given, w):
    rows = 256
    first = lambda width: pl.BlockSpec((rows, width), lambda i: (jnp.minimum(i, 1), 0))
    second = lambda width: pl.BlockSpec((rows, width), lambda i: (jnp.maximum(i - 2, 0), 0))
    tokens = lambda width: pl.BlockSpec((rows, width), lambda i: (i, 0))
    return pl.pallas_call(
        mlp_kernel,
        grid=(1024 // rows,),
        in_specs=[first(D), second(D), first(384), second(384)]
        + [pl.BlockSpec((D, 768), lambda i: (0, 0))],
        out_specs=[tokens(D), tokens(384), tokens(768)],
        out_shape=[
            jax.ShapeDtypeStruct((1024, D), BF),
            jax.ShapeDtypeStruct((1024, 384), BF),
            jax.ShapeDtypeStruct((1024, 768), BF),
        ],
        compiler_params=pltpu.CompilerParams(vmem_limit_bytes=24 * MIB),
        cost_estimate=cost(6.2),
        name="mlp",
    )(own, other, own_given, other_given, w)


def product_of_halves(place, x, near, far):
    total = None
    for side, d in ((place[0], near), (1 - place[0], far)):
        rows = pl.ds(pl.multiple_of(side * 1024, 1024), 1024)
        term = mm_tn(x[rows, :], d[...])
        total = term if total is None else total + term
    return total


def product_of_parts(xs, ds):
    total, start = None, 0
    for n in range(max(len(xs), len(ds))):
        x, d = xs[min(n, len(xs) - 1)], ds[min(n, len(ds) - 1)]
        rows = min(x.shape[0], d.shape[0])
        x = x[pl.ds(start, rows), :] if x.shape[0] > rows else x[...]
        d = d[pl.ds(start, rows), :] if d.shape[0] > rows else d[...]
        term = mm_tn(x, d)
        total = term if total is None else total + term
        start += rows
    return total


def grad_columns_kernel(counts, place, *refs):
    a, b = counts
    gain, w, out, gain_out = refs[a + b :]
    if a == 1:
        total = product_of_halves(place, refs[0], refs[1], refs[2])
    else:
        total = product_of_parts(refs[:a], refs[a : a + b])
    gain_out[...] = jnp.sum(total * w[...].astype(F32), axis=1, keepdims=True)
    columns = jnp.transpose(gain[...])
    lane = lax.broadcasted_iota(jnp.int32, columns.shape, 1) - 2 * pl.program_id(0)
    pick = lambda n: jnp.sum(jnp.where(lane == n, columns, 0.0), axis=1, keepdims=True)
    total = total * jnp.concatenate([pick(0), pick(1)], axis=0)
    for q in range(8):
        for j in range(4):
            piece = total[64 * j + 8 * q : 64 * j + 8 * q + 8]
            groups = [piece[:, g : g + 256] for g in range(0, piece.shape[1], 256)]
            out[q, j] = jnp.concatenate(groups, axis=0).astype(BF)


def grad_columns_call(place, xs, ds, gain, w):
    width = w.shape[1]
    return pl.pallas_call(
        functools.partial(grad_columns_kernel, (len(xs), len(ds))),
        grid_spec=pltpu.PrefetchScalarGridSpec(
            num_scalar_prefetch=1,
            grid=(4,),
            in_specs=[pl.BlockSpec((x.shape[0], 256), lambda t, c: (0, t)) for x in xs]
            + [pl.BlockSpec(d.shape, lambda t, c: (0, 0)) for d in ds]
            + [pl.BlockSpec((8, HD), lambda t, c: (0, 0))]
            + [pl.BlockSpec((256, width), lambda t, c: (t, 0))],
            out_specs=[
                pl.BlockSpec((8, 4, width // 32, 256), lambda t, c: (0, t, 0, 0)),
                pl.BlockSpec((256, 1), lambda t, c: (t, 0)),
            ],
        ),
        out_shape=[
            jax.ShapeDtypeStruct((8, 16, width // 32, 256), BF),
            jax.ShapeDtypeStruct((D, 1), F32),
        ],
        compiler_params=pltpu.CompilerParams(vmem_limit_bytes=24 * MIB),
        cost_estimate=cost(3.4),
        name="grad_columns",
    )(place, *xs, *ds, gain, w)


def rows_kernel(got, out):
    for n in range(8):
        total = got[n].astype(F32) + got[8 + n].astype(F32)
        total = jnp.concatenate([total[0:8], total[8:16], total[16:24]], axis=1)
        for g in range(4):
            out[:, pl.ds(192 * (8 * g + n), 192)] = total[:, 192 * g : 192 * g + 192]


def rows_call(got):
    return pl.pallas_call(
        rows_kernel,
        out_shape=jax.ShapeDtypeStruct((8, 2 * FF), F32),
        compiler_params=pltpu.CompilerParams(vmem_limit_bytes=16 * MIB),
        cost_estimate=cost(1),
        name="rows",
    )(got)


def grad_rows_kernel(counts, *refs):
    a, b = counts
    out = refs[a + b]
    step = out.shape[2] // 2
    total = product_of_parts(refs[:a], refs[a : a + b])
    for q in range(8):
        low, high = q * step, (8 + q) * step
        piece = jnp.concatenate([total[low : low + step], total[high : high + step]], axis=0)
        out[q, 0] = piece.astype(BF)


def grad_rows_call(xs, ds):
    rows = xs[0].shape[1] // 8
    return pl.pallas_call(
        functools.partial(grad_rows_kernel, (len(xs), len(ds))),
        grid=(4,),
        in_specs=[pl.BlockSpec(x.shape, lambda t: (0, 0)) for x in xs]
        + [pl.BlockSpec((d.shape[0], 256), lambda t: (0, t)) for d in ds],
        out_specs=pl.BlockSpec((8, 1, rows, 256), lambda t: (0, t, 0, 0)),
        out_shape=jax.ShapeDtypeStruct((8, 4, rows, 256), BF),
        compiler_params=pltpu.CompilerParams(vmem_limit_bytes=24 * MIB),
        cost_estimate=cost(3),
        name="grad_rows",
    )(*xs, *ds)


def adam(weight, grad, first, second, rate, decay):
    first = BETA_ONE * first + (1.0 - BETA_ONE) * grad
    second = BETA_TWO * second + (1.0 - BETA_TWO) * grad * grad
    ratio = (
        first / (1.0 - BETA_ONE**STEP) / (jnp.sqrt(second / (1.0 - BETA_TWO**STEP)) + ADAM_EPSILON)
    )
    return (first, second, weight - rate * (ratio + decay * weight))


def on_device(
    hidden, cotangent, segments, w_qkv, w_gu, w_o, w_down, norm_gains,
    m_qkv, m_gu, m_o, m_down, m_gains, v_qkv, v_gu, v_o, v_down, v_gains,
):
    core = lax.axis_index("core")
    xhi = lax.axis_index("xhi")
    zero_core = core == 0
    zero_xhi = xhi == 0
    y = lax.axis_index("y")
    z = lax.axis_index("z")
    place = jnp.stack([xhi, core, y]).astype(jnp.int32)

    def by_xhi(own, other, axis=0):
        return jnp.concatenate(
            [jnp.where(zero_xhi, own, other), jnp.where(zero_xhi, other, own)], axis=axis
        )

    def back_by_y(value):
        return jnp.concatenate(
            [lax.dynamic_slice_in_dim(value, (y + 4 - r) % 4, 1, 0) for r in range(4)], axis=0
        )

    masters = (w_qkv, w_gu, w_o, w_down, norm_gains)
    rates = (
        STEP_SCALE / math.sqrt(D),
        STEP_SCALE / math.sqrt(D),
        STEP_SCALE / math.sqrt(H * HD * 4 // KEYS_SEEN),
        STEP_SCALE / math.sqrt(FF),
        GAIN_RATE,
    )
    firsts = (m_qkv, m_gu, m_o, m_down, m_gains)
    seconds = (v_qkv, v_gu, v_o, v_down, v_gains)
    grad_out = cotangent[0]
    low_qkv, low_o, low_down = (w.astype(BF) for w in (w_qkv, w_o, w_down))

    x = hidden[0].astype(F32)
    unit_one, factor_one = normalize(x)
    columns = jnp.concatenate(
        [
            low_qkv[:, : H * HD].reshape(64, 8, 256),
            low_qkv[:, H * HD : (H + KVH) * HD].reshape(64, 8, HD),
            low_qkv[:, (H + KVH) * HD :].reshape(64, 8, HD),
        ],
        axis=-1,
    ).transpose(1, 0, 2)
    columns = jnp.concatenate([columns[:, :32], columns[:, 32:]], axis=-1)
    small = jnp.concatenate(
        [
            norm_gains.astype(BF),
            jnp.zeros((112,), BF),
            segments[0].astype(BF),
            jnp.zeros((640,), BF),
        ]
    )
    small = jnp.concatenate([small[None], jnp.zeros((15, D), BF)], axis=0)
    quarter_o = lax.dynamic_slice_in_dim(low_o, z * 32, 32, 0)
    spread_x = jnp.broadcast_to(unit_one.astype(BF)[None], (8, 128, D))
    same = jnp.concatenate([quarter_o, small], axis=0)
    same = jnp.broadcast_to(same[None], (8, 48, D))
    packet = jnp.concatenate([spread_x, columns, same], axis=1)
    own = all_to_all(packet, CHIPS)
    gu_columns = columns_call(w_gu)
    own, low_down, gu_columns = tie(own, low_down, gu_columns)
    other = swap_core(own)
    small = jnp.stack(
        [
            jnp.where(zero_core, own[:, 192], other[:, 192]),
            jnp.where(zero_core, other[:, 192], own[:, 192]),
        ],
        axis=1,
    ).reshape(16, D)
    gains = small[:, :144].reshape(2304).astype(F32)
    docs = small[:, 256:384].astype(F32)
    gain_attn, gain_mlp = gains[:D], gains[D : 2 * D]
    gain_heads = jnp.concatenate([gains[2 * D :].reshape(2, HD), jnp.zeros((6, HD), F32)], axis=0)
    table = jnp.asarray(rope_table())

    gu_columns = all_to_all(gu_columns, CHIPS)
    far_down = swap_x(low_down)

    sides_o = lax.all_gather(own[:, 160:192], "z", axis=0, tiled=False)
    sides_o, dy_mine = tie(sides_o, grad_out)
    dy_own = lax.all_gather(dy_mine, "y", axis=0, tiled=False)
    unit_all, q, k, v, raw, mixed, total, qx, kx, w_mine, w_back = qkv_call(
        place, own, other, table, gain_attn.reshape(8, HD), gain_heads, docs
    )
    mixed, gu_columns, far_down, low_down = tie(mixed, gu_columns, far_down, low_down)

    got = all_to_all(mixed.reshape(8, 256, HD), CHIPS)

    own_gu = jnp.where(zero_core, gu_columns[:, 0], gu_columns[:, 1])
    other_gu = swap_core(jnp.where(zero_core, gu_columns[:, 1], gu_columns[:, 0]))
    gu, gu_gain = place_call(place, own_gu, other_gu, gain_mlp.reshape(8, HD))
    got, gu, gu_gain = tie(got, gu, gu_gain)

    keep, send = collect_call(place, got, sides_o)
    middle = x + keep + swap_core(send).astype(F32)
    unit_two, factor_two = normalize(middle)
    unit_two_low, w_back, far_down = tie(unit_two.astype(BF), w_back, far_down)

    down = by_xhi(low_down, far_down)
    dy_own = back_by_y(dy_own).reshape(512, D)
    dy_other = swap_core(dy_own)
    inner_grad_own = mm_nt(dy_own, down)
    inner_grad_other = mm_nt(dy_other, down)
    tokens_own = jnp.concatenate(
        [unit_two_low] + [shift_y(unit_two_low, r) for r in range(1, 4)], axis=0
    )
    tokens_own, mixed, w_far, inner_grad_own, inner_grad_other = tie(
        tokens_own, mixed, swap_x(w_back), inner_grad_own, inner_grad_other
    )
    halves = mixed.reshape(2, 1024, HD)
    mixed_keep = jnp.where(zero_xhi, halves[0], halves[1])
    mixed_send = jnp.where(zero_xhi, halves[1], halves[0])
    tokens_other = swap_core(tokens_own)
    part, inner, grad_gu = mlp_call(
        tokens_own, tokens_other, inner_grad_own, inner_grad_other, gu_gain
    )
    part = (part[:512].astype(F32) + swap_core(part[512:]).astype(F32)).astype(BF)

    part, mixed_send, tokens_own, tokens_other, inner, grad_gu = tie(
        part, mixed_send, tokens_own, tokens_other, inner, grad_gu
    )
    shifted = [shift_y(part[128 * r : 128 * r + 128], -r) for r in range(1, 4)]
    sum_gu, gain_mlp_grad = grad_columns_call(
        place, (tokens_own, tokens_other), (grad_gu,), gain_mlp.reshape(8, HD), gu
    )
    sum_down = grad_rows_call((inner,), (dy_own, dy_other))
    packet = jnp.concatenate([sum_gu.reshape(8, 384, 256), sum_down.reshape(8, 192, 256)], axis=1)
    *shifted, packet, mixed_got = tie(*shifted, packet, swap_xhi(mixed_send))
    packet = lax.psum_scatter(packet.reshape(8 * 576, 256), DP, scatter_dimension=0, tiled=True)
    grad_unit_two = part[:128].astype(F32)
    for value in shifted:
        grad_unit_two += value.astype(F32)
    grad_middle = grad_out.astype(F32) + norm_back(grad_unit_two, unit_two, factor_two)
    grad_middle_low = grad_middle.astype(BF)
    grad_middle_half = lax.all_gather(grad_middle_low, YC, axis=0, tiled=True)
    blocks = to_heads_call(place, grad_middle_low, swap_core(grad_middle_low), sides_o)
    blocks, mixed_keep, mixed_got, inner = tie(blocks, mixed_keep, mixed_got, inner)
    grad_mixed = all_to_all(blocks, CHIPS).reshape(SEQLEN, HD)
    mixed_pair = by_xhi(mixed_keep, mixed_got, axis=1)
    out_part = mm(inner[:512], down) + swap_core(mm(inner[512:], down).astype(BF)).astype(F32)
    out_part = out_part.astype(BF)
    out_part = back_by_y(out_part.reshape(4, 128, D)).reshape(512, D)
    grad_mixed, mixed_pair, out_part = tie(grad_mixed, mixed_pair, out_part)

    dq, keep, send, gain_part = attend_back_call(
        place, q, qx, k, kx, v, mixed, total, gain_heads, grad_mixed, raw, table
    )
    dq, keep, send, packet = tie(dq, keep, send, packet)

    near, far = join_call(place, dq, keep, swap_core(send))
    near, far, packet = tie(near, far, packet)
    parts_gu = all_to_all(packet[:384].reshape(16, 24, 256), SEQ)
    rows_down = packet[384:].reshape(4, 2, 24, 256)
    kept = jnp.where(zero_xhi, rows_down[:, 0], rows_down[:, 1]).astype(F32)
    came = swap_xhi(jnp.where(zero_xhi, rows_down[:, 1], rows_down[:, 0]))
    sum_heads, gain_attn_grad = grad_columns_call(
        place, (unit_all,), (near, far), gain_attn.reshape(8, HD), w_mine
    )
    far = swap_xhi(far)
    sum_heads, mixed_pair = tie(sum_heads, mixed_pair)
    sum_o = grad_rows_call((mixed_pair,), (grad_middle_half,))
    sum_gains = jnp.concatenate(
        [gain_attn_grad[:, 0], gain_mlp_grad[:, 0], gain_part[0], gain_part[1]]
    ).astype(BF)
    sum_gains = jnp.pad(sum_gains.reshape(9, 256), ((0, 7), (0, 0)))
    sums = jnp.concatenate(
        [
            sum_heads.reshape(8, 128, 256),
            sum_o.reshape(8, 128, 256),
            jnp.broadcast_to(sum_gains[None], (8, 16, 256)),
        ],
        axis=1,
    )
    sums, parts_gu, came, far = tie(sums, parts_gu, came, far)
    sums = all_to_all(sums, DP)
    rows_gu = rows_call(parts_gu)
    rows_down = (kept + came.astype(F32)).transpose(1, 0, 2).reshape(24, D)
    wide = jnp.concatenate([rows_gu, rows_down.reshape(8, 3 * D)], axis=1).astype(BF)
    near, far, wide = tie(near, far, wide)
    wide = lax.all_gather(wide, DP, axis=0, tiled=True)
    mine, theirs = back_call(place, near, far, w_back, w_far)
    sums, mine, theirs, out_part = tie(sums, mine, theirs, out_part)
    output = lax.psum_scatter(out_part, "y", scatter_dimension=0, tiled=True)
    output = middle + output.astype(F32)
    sums = sums.astype(F32).sum(axis=0).astype(BF)
    sum_gains = jnp.pad(sums[256:265].reshape(16, 1, 144), ((0, 0), (0, 7), (0, 112)))
    parts = jnp.concatenate([sums[:128].reshape(16, 8, 256), sum_gains], axis=1)
    rows_o = sums[128:256].reshape(4, 2, 16, 256)
    parts = all_to_all(parts, SEQ)
    blocks = merge_call(place, mine, swap_core(theirs))
    parts, *blocks = tie(parts, *blocks)
    blocks = [blocks[0]] + [shift_y(blocks[n], n) for n in range(1, 4)]
    kept = jnp.where(zero_xhi, rows_o[:, 0], rows_o[:, 1]).astype(F32)
    came = swap_xhi(jnp.where(zero_xhi, rows_o[:, 1], rows_o[:, 0])).astype(F32)
    rows_o = (kept + came).transpose(1, 0, 2).reshape(16, D).astype(BF)
    grad_gains = parts[:, 8, :144].astype(F32).sum(axis=0)
    pick = lambda block: block.transpose(1, 0, 2).reshape(8, -1)
    pairs = parts[:, :8, HD:].reshape(8, 2, 8, HD)
    rows_qkv = jnp.concatenate(
        [pick(parts[:, :8, :HD]), pick(pairs[:, 0]), pick(pairs[:, 1])], axis=1
    )

    last = jnp.concatenate(
        [rows_qkv.reshape(8, 4, D).transpose(1, 0, 2).reshape(32, D), rows_o], axis=0
    )
    last = spread(last, DP, 8)
    updates = {}
    for index, grad in ((1, wide[:, : 2 * FF]), (3, wide[:, 2 * FF :].reshape(192, D))):
        updates[index] = adam(
            masters[index], grad.astype(F32), firsts[index], seconds[index], rates[index], DECAY
        )
    last, updates[1], updates[3] = tie(last, updates[1], updates[3])
    total_back = blocks[0].astype(F32)
    for value in blocks[1:]:
        total_back += value.astype(F32)
    hidden_grad = grad_middle + norm_back(total_back, unit_one, factor_one)
    owned_qkv = last[:, :32].reshape(8, 4, 8, D).transpose(0, 2, 1, 3).reshape(64, 4096)
    owned_o = last[:, 32:].reshape(128, D)
    results = [output.astype(BF)[None], hidden_grad[None]]
    for index, grad, decay in ((0, owned_qkv, DECAY), (2, owned_o, DECAY), (4, grad_gains, 0.0)):
        updates[index] = adam(
            masters[index], grad.astype(F32), firsts[index], seconds[index], rates[index], decay
        )
    for index in range(5):
        results.extend(updates[index])
    return tuple(results)


def solution(mesh):
    fine = Mesh(mesh.devices.reshape(2, 4, 2, 4, 2), ("xlo", "z", "xhi", "y", "core"))
    tokens = P(DP, SEQ, None)
    rows = P(SEQ, None)
    return jax.shard_map(
        on_device,
        mesh=fine,
        in_specs=(tokens, tokens, P(DP, SEQ))
        + (rows, rows, rows, rows, P(SEQ)) * 3,
        out_specs=(tokens, tokens) + (rows,) * 12 + (P(SEQ),) * 3,
        check_vma=False,
    )
```

```python
import functools
import math

import jax
import jax.numpy as jnp
import numpy as np
from jax import lax
from jax.experimental import pallas as pl
from jax.experimental.pallas import tpu as pltpu
from jax.sharding import Mesh
from jax.sharding import PartitionSpec as P

D = 1024
H = 16
KVH = 8
HD = 128
FF = 3072
KEYS_SEEN = 512
STEP = 10
SEQLEN = 2048
EPSILON = 1e-06
THETA = 1000000.0
BETA_ONE = 0.9
BETA_TWO = 0.95
ADAM_EPSILON = 1e-08
DECAY = 0.1
STEP_SCALE = 1.5
GAIN_RATE = 0.8

SCALE = HD**-0.5
LOG2E = math.log2(math.e)
FAR = 1024.0
BLK = 512

DP = ("xlo", "z")
SEQ = ("xhi", "y", "core")
CHIPS = ("xhi", "y")
YC = ("y", "core")
ALL = DP + SEQ
MIB = 1024 * 1024
BF = jnp.bfloat16
F32 = jnp.float32


def mm(a, b):
    return jnp.dot(a, b, preferred_element_type=F32)


def mm_nt(a, b):
    return lax.dot_general(a, b, (((1,), (1,)), ((), ())), preferred_element_type=F32)


def mm_tn(a, b):
    return lax.dot_general(a, b, (((0,), (0,)), ((), ())), preferred_element_type=F32)


def normalize(value):
    factor = lax.rsqrt(jnp.mean(value * value, axis=-1, keepdims=True) + EPSILON)
    return value * factor, factor


def norm_back(grad_unit, unit, factor):
    return factor * (grad_unit - unit * jnp.mean(grad_unit * unit, axis=-1, keepdims=True))


def rope_table():
    freq = np.float32(THETA) ** (-np.arange(0, HD, 2).astype(np.float32) / np.float32(HD))
    angle = np.arange(SEQLEN, dtype=np.float32)[:, None] * freq.astype(np.float32)[None, :]
    return np.concatenate([np.cos(angle), np.sin(angle)], 1).astype(np.float32)


def swap_core(value):
    return lax.ppermute(value, "core", [(0, 1), (1, 0)])


def swap_x(value):
    return lax.ppermute(value, ("xlo", "xhi"), [(0, 3), (3, 0), (1, 2), (2, 1)])


def swap_xhi(value):
    return lax.ppermute(value, "xhi", [(0, 1), (1, 0)])


def all_to_all(value, axes):
    return lax.all_to_all(value, axes, split_axis=0, concat_axis=0, tiled=True)


def shift_y(value, by):
    return lax.ppermute(value, "y", [(n, (n + by) % 4) for n in range(4)])


def shift_chips(value, dx, dy):
    pairs = [(4 * a + b, 4 * (a ^ dx) + (b + dy) % 4) for a in range(2) for b in range(4)]
    return lax.ppermute(value, CHIPS, pairs)


def tie(*values):
    return lax.optimization_barrier(values)


def spread(value, axes, count):
    return all_to_all(jnp.broadcast_to(value[None], (count, *value.shape)), axes)


def cost(us):
    return pl.CostEstimate(
        flops=int(us * 1.1e9), bytes_accessed=int(us * 2e6), transcendentals=0
    )


SCALARS = pl.BlockSpec(memory_space=pltpu.SMEM)
WHOLE = pl.BlockSpec(memory_space=pltpu.VMEM)


def gather_weights(place, own, other, gain, w, mine_out, back_out):
    first = place[1] == 0
    columns = jnp.transpose(gain[...])
    for p in range(8):
        for c in range(2):
            block = jnp.where(first == (c == 0), own[p], other[p])
            for half in range(2):
                start = (2 * p + c) * 64 + half * 32
                rows = pl.ds(start, 32)
                at = half * 512
                query = jnp.where(first, block[:, at : at + HD], block[:, at + HD : at + 2 * HD])
                key = block[:, at + 2 * HD : at + 3 * HD]
                value = block[:, at + 3 * HD : at + 4 * HD]
                column = columns[start % 128 : start % 128 + 32, start // 128 : start // 128 + 1]
                heads = jnp.concatenate([query, key, value], axis=1).astype(F32) * column
                w[rows, :] = heads.astype(BF)
                mine = jnp.concatenate([query, jnp.where(first, key, value)], axis=1)
                mine_out[rows, :] = mine
                back_out[rows, :] = (mine.astype(F32) * column).astype(BF)


def document_columns(docs, qx, kx):
    columns = jnp.transpose(docs[...])
    lane = lax.broadcasted_iota(jnp.int32, (128, HD), 1)
    for n in range(16):
        rows = pl.ds(128 * n, 128)
        same = columns[:, n : n + 1] == lane.astype(F32)
        qx[rows, :] = jnp.where(same & (lane < 8), -FAR, 0.0).astype(BF)
        kx[rows, :] = jnp.where(same | (lane >= 16), 0.0, 1.0).astype(BF)


def qkv_kernel(
    place, own, other, own_w, other_w, table, gain, gains, docs,
    x_out, q_out, k_out, v_out, raw_out, out, total, qx, kx, mine_out, back_out, q, k, v, w,
):
    step = pl.program_id(0)
    first = place[1] == 0

    @pl.when(step == 0)
    def _():
        gather_weights(place, own_w, other_w, gain, w, mine_out, back_out)
        document_columns(docs, qx, kx)

    x = []
    for n in range(2):
        a, b = own[n], other[n]
        x += [jnp.where(first, a, b), jnp.where(first, b, a)]
    x = jnp.concatenate(x, axis=0)
    x_out[...] = x
    qkv = mm(x, w[...])
    raw_out[...] = qkv[:, : 2 * HD]
    cos, sin = unpack_table(table[...])
    rows = pl.ds(pl.multiple_of(step * 512, 512), 512)

    def rotated(part, gain):
        unit, _ = normalize(part)
        value = unit * gain
        return value * cos + pltpu.roll(value, HD // 2, 1) * sin

    query = (rotated(qkv[:, :HD], gains[0:1, :]) * (SCALE * LOG2E)).astype(BF)
    key = rotated(qkv[:, HD : 2 * HD], gains[1:2, :]).astype(BF)
    value = qkv[:, 2 * HD :].astype(BF)
    q_out[...] = query
    k_out[...] = key
    v_out[...] = value
    q[rows, :] = query
    k[rows, :] = key
    v[rows, :] = value

    @pl.when(step == SEQLEN // 512 - 1)
    def _():
        attend(q, qx, k, kx, v, out, total)


def attend(q, qx, k, kx, v, out, total):
    ones = jnp.ones((BLK, HD), BF)
    causal = lax.broadcasted_iota(jnp.int32, (BLK, BLK), 1) <= lax.broadcasted_iota(
        jnp.int32, (BLK, BLK), 0
    )
    for i in range(SEQLEN // BLK):
        rows = pl.ds(i * BLK, BLK)
        query = jnp.concatenate([q[rows, :], qx[rows, :]], axis=1)
        acc = None
        for j in range(i + 1):
            cols = pl.ds(j * BLK, BLK)
            key = jnp.concatenate([k[cols, :], kx[cols, :]], axis=1)
            prob = jnp.exp2(mm_nt(query, key))
            if i == j:
                prob = jnp.where(causal, prob, 0.0)
            term = mm(prob.astype(BF), jnp.concatenate([v[cols, :], ones], axis=1))
            acc = term if acc is None else acc + term
        total[rows, :] = acc[:, HD:]
        out[rows, :] = (acc[:, :HD] / acc[:, HD:]).astype(BF)


def unpack_table(table):
    low = lax.broadcasted_iota(jnp.int32, table.shape, 1) < HD // 2
    turned = pltpu.roll(table, HD // 2, 1)
    return jnp.where(low, table, turned), jnp.where(low, -turned, table)


def qkv_call(place, own, other, table, gain, gains, docs):
    rows = 512
    part = pl.BlockSpec((2, 128, D), lambda p, c: (p, 0, 0))
    weights = pl.BlockSpec((8, 32, D), lambda p, c: (0, 4, 0))
    whole = lambda shape: pl.BlockSpec(shape, lambda p, c: (0, 0))
    tokens = lambda width: pl.BlockSpec((rows, width), lambda p, c: (p, 0))
    heads = jax.ShapeDtypeStruct((SEQLEN, HD), BF)
    columns = jax.ShapeDtypeStruct((D, 256), BF)
    return pl.pallas_call(
        qkv_kernel,
        grid_spec=pltpu.PrefetchScalarGridSpec(
            num_scalar_prefetch=1,
            grid=(SEQLEN // rows,),
            in_specs=[part, part, weights, weights, tokens(HD)]
            + [whole((8, HD)), whole((8, HD)), whole((16, HD))],
            out_specs=[tokens(D), tokens(HD), tokens(HD), tokens(HD), tokens(2 * HD)]
            + [whole((SEQLEN, HD))] * 4
            + [whole((D, 256))] * 2,
            scratch_shapes=[pltpu.VMEM((SEQLEN, HD), BF)] * 3 + [pltpu.VMEM((D, 384), BF)],
        ),
        out_shape=[
            jax.ShapeDtypeStruct((SEQLEN, D), BF),
            heads,
            heads,
            heads,
            jax.ShapeDtypeStruct((SEQLEN, 2 * HD), F32),
            heads,
            jax.ShapeDtypeStruct((SEQLEN, HD), F32),
            heads,
            heads,
            columns,
            columns,
        ],
        compiler_params=pltpu.CompilerParams(vmem_limit_bytes=58 * MIB),
        cost_estimate=cost(14),
        name="qkv_attend",
    )(place, own, other, own, other, table, gain, gains, docs)


def thirds(value):
    high = value.astype(BF).astype(F32)
    middle = (value - high).astype(BF).astype(F32)
    return high, middle, value - high - middle


def attend_back_kernel(
    place, q, qx, k, kx, v, out, total, gains, grad, raw_hbm, table_hbm,
    dq_out, keep_out, send_out, gain_out, qx_s, gx_s, dq_s, raw, table, sems,
):
    first = place[1] == 0
    late = [
        pltpu.make_async_copy(a, b, sems.at[n])
        for n, (a, b) in enumerate(((raw_hbm, raw), (table_hbm, table)))
    ]
    for copy in late:
        copy.start()
    count = SEQLEN // BLK
    lane = lax.broadcasted_iota(jnp.int32, (BLK, HD), 1)
    ones = jnp.ones((BLK, HD), BF)
    causal = lax.broadcasted_iota(jnp.int32, (BLK, BLK), 0) <= lax.broadcasted_iota(
        jnp.int32, (BLK, BLK), 1
    )

    def placed(parts, start):
        value = jnp.zeros((BLK, HD), F32)
        for n, part in enumerate(parts):
            value = jnp.where(lane == start + n, part, value)
        return value

    for i in range(count):
        rows = pl.ds(i * BLK, BLK)
        level = placed(thirds(jnp.log2(total[rows, :])), 8)
        qx_s[rows, :] = (qx[rows, :].astype(F32) - level).astype(BF)
        delta = jnp.sum(grad[rows, :].astype(F32) * out[rows, :].astype(F32), 1, keepdims=True)
        gx_s[rows, :] = (-placed(thirds(delta), 0)).astype(BF)

    def back(value, part, gain, rows):
        cos, sin = unpack_table(table[rows, :])
        turned = value * cos - pltpu.roll(value, HD // 2, 1) * sin
        unit, factor = normalize(raw[rows, pl.ds(part * HD, HD)])
        return (
            norm_back(turned * gain, unit, factor),
            jnp.sum(turned * unit, axis=0, keepdims=True),
        )

    gain_q = jnp.zeros((1, HD), F32)
    gain_k = jnp.zeros((1, HD), F32)
    for j in range(count):
        cols = pl.ds(j * BLK, BLK)
        key = jnp.concatenate([k[cols, :], kx[cols, :]], axis=1)
        value = jnp.concatenate([v[cols, :], ones], axis=1)
        dk = dv = None
        for i in range(j, count):
            rows = pl.ds(i * BLK, BLK)
            query = jnp.concatenate([q[rows, :], qx_s[rows, :]], axis=1)
            given = jnp.concatenate([grad[rows, :], gx_s[rows, :]], axis=1)
            prob = jnp.exp2(mm_nt(key, query))
            if i == j:
                prob = jnp.where(causal, prob, 0.0)
            score = (prob * mm_nt(value, given)).astype(BF)
            dv_term = mm(prob.astype(BF), grad[rows, :])
            dk_term = mm(score, q[rows, :])
            dq_term = mm_tn(score, k[cols, :])
            dv = dv_term if dv is None else dv + dv_term
            dk = dk_term if dk is None else dk + dk_term
            if j == 0:
                dq_s[rows, :] = dq_term
            else:
                dq_s[rows, :] += dq_term
        if j == 0:
            for copy in late:
                copy.wait()
        dk, gain = back(dk * (1.0 / LOG2E), 1, gains[1:2, :], cols)
        keep_out[cols, :] = jnp.where(first, dk, dv).astype(BF)
        send_out[cols, :] = jnp.where(first, dv, dk).astype(BF)
        gain_k += gain
        dq, gain = back(dq_s[cols, :] * SCALE, 0, gains[0:1, :], cols)
        dq_out[cols, :] = dq.astype(BF)
        gain_q += gain
    gain_out[...] = jnp.concatenate([gain_q, gain_k, jnp.zeros((6, HD), F32)], axis=0)


def attend_back_call(*args):
    tokens = jax.ShapeDtypeStruct((SEQLEN, HD), BF)
    return pl.pallas_call(
        attend_back_kernel,
        out_shape=[tokens, tokens, tokens, jax.ShapeDtypeStruct((8, HD), F32)],
        in_specs=[SCALARS]
        + [WHOLE] * (len(args) - 3)
        + [pl.BlockSpec(memory_space=pl.ANY)] * 2,
        scratch_shapes=[
            pltpu.VMEM((SEQLEN, HD), BF),
            pltpu.VMEM((SEQLEN, HD), BF),
            pltpu.VMEM((SEQLEN, HD), F32),
            pltpu.VMEM((SEQLEN, 2 * HD), F32),
            pltpu.VMEM((SEQLEN, HD), F32),
            pltpu.SemaphoreType.DMA((2,)),
        ],
        compiler_params=pltpu.CompilerParams(vmem_limit_bytes=58 * MIB),
        cost_estimate=cost(12),
        name="attend_back",
    )(*args)


def columns_kernel(w, out):
    for n in range(8):
        for g in range(4):
            part = w[:, pl.ds(192 * (8 * g + n), 192)].astype(BF)
            out[n // 2, n % 2, :, pl.ds(192 * g, 192)] = part
            out[4 + n // 2, n % 2, :, pl.ds(192 * g, 192)] = part


def columns_call(w):
    return pl.pallas_call(
        columns_kernel,
        out_shape=jax.ShapeDtypeStruct((8, 2, 64, 768), BF),
        compiler_params=pltpu.CompilerParams(vmem_limit_bytes=16 * MIB),
        cost_estimate=cost(1),
        name="columns",
    )(w)


def place_kernel(place, own, other, gain, raw_out, gained_out):
    columns = jnp.transpose(gain[...])
    first = place[1] == 0
    for p in range(8):
        for c in range(2):
            rows = pl.ds((2 * p + c) * 64, 64)
            block = jnp.where(first == (c == 0), own[p], other[p])
            raw_out[rows, :] = block
            column = columns[64 * c : 64 * c + 64, p : p + 1]
            gained_out[rows, :] = (block.astype(F32) * column).astype(BF)


def place_call(place, own, other, gain):
    return pl.pallas_call(
        place_kernel,
        out_shape=[jax.ShapeDtypeStruct((D, 768), BF)] * 2,
        in_specs=[SCALARS, WHOLE, WHOLE, WHOLE],
        compiler_params=pltpu.CompilerParams(vmem_limit_bytes=24 * MIB),
        cost_estimate=cost(1.5),
        name="place",
    )(place, own, other, gain)


def collect_kernel(place, got, w, keep_out, send_out):
    def rows_of(c):
        rows = pl.ds(pl.multiple_of(c * 128, 128), 128)
        left = jnp.concatenate([got[n, rows, :] for n in range(8)], axis=1)
        right = jnp.concatenate([w[quarter, n] for n in range(8) for quarter in range(4)], axis=0)
        return mm(left, right)

    send_out[...] = rows_of(1 - place[1]).astype(BF)
    keep_out[...] = rows_of(place[1])


def collect_call(place, got, w):
    return pl.pallas_call(
        collect_kernel,
        out_shape=[jax.ShapeDtypeStruct((128, D), F32), jax.ShapeDtypeStruct((128, D), BF)],
        in_specs=[SCALARS, WHOLE, WHOLE],
        compiler_params=pltpu.CompilerParams(vmem_limit_bytes=32 * MIB),
        cost_estimate=cost(2),
        name="collect",
    )(place, got, w)


def to_heads_kernel(place, mine, others, w, out):
    core = place[1]
    for c, value in ((core, mine), (1 - core, others)):
        rows = pl.ds(pl.multiple_of(c * 128, 128), 128)
        for n in range(8):
            right = jnp.concatenate([w[quarter, n] for quarter in range(4)], axis=0)
            out[n, rows, :] = mm_nt(value[...], right).astype(BF)


def to_heads_call(*args):
    return pl.pallas_call(
        to_heads_kernel,
        out_shape=jax.ShapeDtypeStruct((8, 256, HD), BF),
        in_specs=[SCALARS] + [WHOLE] * 3,
        compiler_params=pltpu.CompilerParams(vmem_limit_bytes=16 * MIB),
        cost_estimate=cost(2),
        name="to_heads",
    )(*args)


def join_kernel(place, query, keep, got, near_out, far_out):
    for side, out in ((place[0], near_out), (1 - place[0], far_out)):
        rows = pl.ds(pl.multiple_of(side * 1024, 1024), 1024)
        total = keep[rows, :].astype(F32) + got[rows, :].astype(F32)
        out[...] = jnp.concatenate([query[rows, :], total.astype(BF)], axis=1)


def join_call(*args):
    half = jax.ShapeDtypeStruct((1024, 256), BF)
    return pl.pallas_call(
        join_kernel,
        out_shape=[half, half],
        in_specs=[SCALARS] + [WHOLE] * 3,
        compiler_params=pltpu.CompilerParams(vmem_limit_bytes=24 * MIB),
        cost_estimate=cost(1.5),
        name="join",
    )(*args)


def back_kernel(place, near, far, w_near, w_far, keep_out, send_out):
    first = place[1] == 0
    part = mm_nt(near[...], w_near[...]) + mm_nt(far[...], w_far[...])
    part = part.astype(BF)
    keep_out[0] = jnp.where(first, part[:128], part[128:])
    send_out[0] = jnp.where(first, part[128:], part[:128])


def back_call(place, near, far, w_near, w_far):
    tokens = pl.BlockSpec((256, 256), lambda p, c: (p, 0))
    whole = pl.BlockSpec((D, 256), lambda p, c: (0, 0))
    chip = pl.BlockSpec((1, 128, D), lambda p, c: (p, 0, 0))
    return pl.pallas_call(
        back_kernel,
        grid_spec=pltpu.PrefetchScalarGridSpec(
            num_scalar_prefetch=1,
            grid=(4,),
            in_specs=[tokens, tokens, whole, whole],
            out_specs=[chip, chip],
        ),
        out_shape=[jax.ShapeDtypeStruct((4, 128, D), BF)] * 2,
        compiler_params=pltpu.CompilerParams(vmem_limit_bytes=24 * MIB),
        cost_estimate=cost(3),
        name="back",
    )(place, near, far, w_near, w_far)


def merge_kernel(place, keep, got, *outs):
    for dy in range(4):
        n = lax.rem(place[2] + dy, 4)
        outs[dy][...] = (keep[n].astype(F32) + got[n].astype(F32)).astype(BF)


def merge_call(*args):
    return pl.pallas_call(
        merge_kernel,
        out_shape=[jax.ShapeDtypeStruct((128, D), BF)] * 4,
        in_specs=[SCALARS] + [WHOLE] * 2,
        compiler_params=pltpu.CompilerParams(vmem_limit_bytes=24 * MIB),
        cost_estimate=cost(1),
        name="merge",
    )(*args)


def mlp_kernel(own, other, own_given, other_given, w, part_out, inner_out, grad_out):
    mine = pl.program_id(0) < 2
    x = jnp.where(mine, own[...], other[...])
    given = jnp.where(mine, own_given[...], other_given[...])
    gate_up = mm(x, w[...])
    gate, up = gate_up[:, :384], gate_up[:, 384:]
    sigmoid = jax.nn.sigmoid(gate)
    silu = gate * sigmoid
    inner_out[...] = (silu * up).astype(BF)
    grad_gate = given * up * sigmoid * (1.0 + gate * (1.0 - sigmoid))
    grad = jnp.concatenate([grad_gate, given * silu], axis=1).astype(BF)
    grad_out[...] = grad
    part_out[...] = mm_nt(grad, w[...]).astype(BF)


def mlp_call(own, other, own_given, other_given, w):
    rows = 256
    first = lambda width: pl.BlockSpec((rows, width), lambda i: (jnp.minimum(i, 1), 0))
    second = lambda width: pl.BlockSpec((rows, width), lambda i: (jnp.maximum(i - 2, 0), 0))
    tokens = lambda width: pl.BlockSpec((rows, width), lambda i: (i, 0))
    return pl.pallas_call(
        mlp_kernel,
        grid=(1024 // rows,),
        in_specs=[first(D), second(D), first(384), second(384)]
        + [pl.BlockSpec((D, 768), lambda i: (0, 0))],
        out_specs=[tokens(D), tokens(384), tokens(768)],
        out_shape=[
            jax.ShapeDtypeStruct((1024, D), BF),
            jax.ShapeDtypeStruct((1024, 384), BF),
            jax.ShapeDtypeStruct((1024, 768), BF),
        ],
        compiler_params=pltpu.CompilerParams(vmem_limit_bytes=24 * MIB),
        cost_estimate=cost(6.2),
        name="mlp",
    )(own, other, own_given, other_given, w)


def product_of_halves(place, x, near, far):
    total = None
    for side, d in ((place[0], near), (1 - place[0], far)):
        rows = pl.ds(pl.multiple_of(side * 1024, 1024), 1024)
        term = mm_tn(x[rows, :], d[...])
        total = term if total is None else total + term
    return total


def product_of_parts(xs, ds):
    total, start = None, 0
    for n in range(max(len(xs), len(ds))):
        x, d = xs[min(n, len(xs) - 1)], ds[min(n, len(ds) - 1)]
        rows = min(x.shape[0], d.shape[0])
        x = x[pl.ds(start, rows), :] if x.shape[0] > rows else x[...]
        d = d[pl.ds(start, rows), :] if d.shape[0] > rows else d[...]
        term = mm_tn(x, d)
        total = term if total is None else total + term
        start += rows
    return total


def grad_columns_kernel(counts, place, *refs):
    a, b = counts
    gain, w, out, gain_out = refs[a + b :]
    if a == 1:
        total = product_of_halves(place, refs[0], refs[1], refs[2])
    else:
        total = product_of_parts(refs[:a], refs[a : a + b])
    gain_out[...] = jnp.sum(total * w[...].astype(F32), axis=1, keepdims=True)
    columns = jnp.transpose(gain[...])
    lane = lax.broadcasted_iota(jnp.int32, columns.shape, 1) - 2 * pl.program_id(0)
    pick = lambda n: jnp.sum(jnp.where(lane == n, columns, 0.0), axis=1, keepdims=True)
    total = total * jnp.concatenate([pick(0), pick(1)], axis=0)
    for q in range(8):
        for j in range(4):
            piece = total[64 * j + 8 * q : 64 * j + 8 * q + 8]
            groups = [piece[:, g : g + 256] for g in range(0, piece.shape[1], 256)]
            out[q, j] = jnp.concatenate(groups, axis=0).astype(BF)


def grad_columns_call(place, xs, ds, gain, w):
    width = w.shape[1]
    return pl.pallas_call(
        functools.partial(grad_columns_kernel, (len(xs), len(ds))),
        grid_spec=pltpu.PrefetchScalarGridSpec(
            num_scalar_prefetch=1,
            grid=(4,),
            in_specs=[pl.BlockSpec((x.shape[0], 256), lambda t, c: (0, t)) for x in xs]
            + [pl.BlockSpec(d.shape, lambda t, c: (0, 0)) for d in ds]
            + [pl.BlockSpec((8, HD), lambda t, c: (0, 0))]
            + [pl.BlockSpec((256, width), lambda t, c: (t, 0))],
            out_specs=[
                pl.BlockSpec((8, 4, width // 32, 256), lambda t, c: (0, t, 0, 0)),
                pl.BlockSpec((256, 1), lambda t, c: (t, 0)),
            ],
        ),
        out_shape=[
            jax.ShapeDtypeStruct((8, 16, width // 32, 256), BF),
            jax.ShapeDtypeStruct((D, 1), F32),
        ],
        compiler_params=pltpu.CompilerParams(vmem_limit_bytes=24 * MIB),
        cost_estimate=cost(3.4),
        name="grad_columns",
    )(place, *xs, *ds, gain, w)


def rows_kernel(got, out):
    for n in range(8):
        total = got[n].astype(F32) + got[8 + n].astype(F32)
        total = jnp.concatenate([total[0:8], total[8:16], total[16:24]], axis=1)
        for g in range(4):
            out[:, pl.ds(192 * (8 * g + n), 192)] = total[:, 192 * g : 192 * g + 192]


def rows_call(got):
    return pl.pallas_call(
        rows_kernel,
        out_shape=jax.ShapeDtypeStruct((8, 2 * FF), F32),
        compiler_params=pltpu.CompilerParams(vmem_limit_bytes=16 * MIB),
        cost_estimate=cost(1),
        name="rows",
    )(got)


def grad_rows_kernel(counts, *refs):
    a, b = counts
    out = refs[a + b]
    step = out.shape[2] // 2
    total = product_of_parts(refs[:a], refs[a : a + b])
    for q in range(8):
        low, high = q * step, (8 + q) * step
        piece = jnp.concatenate([total[low : low + step], total[high : high + step]], axis=0)
        out[q, 0] = piece.astype(BF)


def grad_rows_call(xs, ds):
    rows = xs[0].shape[1] // 8
    return pl.pallas_call(
        functools.partial(grad_rows_kernel, (len(xs), len(ds))),
        grid=(4,),
        in_specs=[pl.BlockSpec(x.shape, lambda t: (0, 0)) for x in xs]
        + [pl.BlockSpec((d.shape[0], 256), lambda t: (0, t)) for d in ds],
        out_specs=pl.BlockSpec((8, 1, rows, 256), lambda t: (0, t, 0, 0)),
        out_shape=jax.ShapeDtypeStruct((8, 4, rows, 256), BF),
        compiler_params=pltpu.CompilerParams(vmem_limit_bytes=24 * MIB),
        cost_estimate=cost(3),
        name="grad_rows",
    )(*xs, *ds)


def adam(weight, grad, first, second, rate, decay):
    first = BETA_ONE * first + (1.0 - BETA_ONE) * grad
    second = BETA_TWO * second + (1.0 - BETA_TWO) * grad * grad
    ratio = (
        first / (1.0 - BETA_ONE**STEP) / (jnp.sqrt(second / (1.0 - BETA_TWO**STEP)) + ADAM_EPSILON)
    )
    return (first, second, weight - rate * (ratio + decay * weight))


def on_device(
    hidden, cotangent, segments, w_qkv, w_gu, w_o, w_down, norm_gains,
    m_qkv, m_gu, m_o, m_down, m_gains, v_qkv, v_gu, v_o, v_down, v_gains,
):
    core = lax.axis_index("core")
    xhi = lax.axis_index("xhi")
    zero_core = core == 0
    zero_xhi = xhi == 0
    y = lax.axis_index("y")
    z = lax.axis_index("z")
    place = jnp.stack([xhi, core, y]).astype(jnp.int32)

    def by_xhi(own, other, axis=0):
        return jnp.concatenate(
            [jnp.where(zero_xhi, own, other), jnp.where(zero_xhi, other, own)], axis=axis
        )

    def back_by_y(value):
        return jnp.concatenate(
            [lax.dynamic_slice_in_dim(value, (y + 4 - r) % 4, 1, 0) for r in range(4)], axis=0
        )

    masters = (w_qkv, w_gu, w_o, w_down, norm_gains)
    rates = (
        STEP_SCALE / math.sqrt(D),
        STEP_SCALE / math.sqrt(D),
        STEP_SCALE / math.sqrt(H * HD * 4 // KEYS_SEEN),
        STEP_SCALE / math.sqrt(FF),
        GAIN_RATE,
    )
    firsts = (m_qkv, m_gu, m_o, m_down, m_gains)
    seconds = (v_qkv, v_gu, v_o, v_down, v_gains)
    grad_out = cotangent[0]
    low_qkv, low_o, low_down = (w.astype(BF) for w in (w_qkv, w_o, w_down))

    x = hidden[0].astype(F32)
    unit_one, factor_one = normalize(x)
    columns = jnp.concatenate(
        [
            low_qkv[:, : H * HD].reshape(64, 8, 256),
            low_qkv[:, H * HD : (H + KVH) * HD].reshape(64, 8, HD),
            low_qkv[:, (H + KVH) * HD :].reshape(64, 8, HD),
        ],
        axis=-1,
    ).transpose(1, 0, 2)
    columns = jnp.concatenate([columns[:, :32], columns[:, 32:]], axis=-1)
    small = jnp.concatenate(
        [
            norm_gains.astype(BF),
            jnp.zeros((112,), BF),
            segments[0].astype(BF),
            jnp.zeros((640,), BF),
        ]
    )
    small = jnp.concatenate([small[None], jnp.zeros((15, D), BF)], axis=0)
    quarter_o = lax.dynamic_slice_in_dim(low_o, z * 32, 32, 0)
    spread_x = jnp.broadcast_to(unit_one.astype(BF)[None], (8, 128, D))
    same = jnp.concatenate([quarter_o, small], axis=0)
    same = jnp.broadcast_to(same[None], (8, 48, D))
    packet = jnp.concatenate([spread_x, columns, same], axis=1)
    own = all_to_all(packet, CHIPS)
    gu_columns = columns_call(w_gu)
    own, low_down, gu_columns = tie(own, low_down, gu_columns)
    other = swap_core(own)
    small = jnp.stack(
        [
            jnp.where(zero_core, own[:, 192], other[:, 192]),
            jnp.where(zero_core, other[:, 192], own[:, 192]),
        ],
        axis=1,
    ).reshape(16, D)
    gains = small[:, :144].reshape(2304).astype(F32)
    docs = small[:, 256:384].astype(F32)
    gain_attn, gain_mlp = gains[:D], gains[D : 2 * D]
    gain_heads = jnp.concatenate([gains[2 * D :].reshape(2, HD), jnp.zeros((6, HD), F32)], axis=0)
    table = jnp.asarray(rope_table())

    gu_columns = all_to_all(gu_columns, CHIPS)
    far_down = swap_x(low_down)

    sides_o = lax.all_gather(own[:, 160:192], "z", axis=0, tiled=False)
    sides_o, dy_mine = tie(sides_o, grad_out)
    dy_own = lax.all_gather(dy_mine, "y", axis=0, tiled=False)
    unit_all, q, k, v, raw, mixed, total, qx, kx, w_mine, w_back = qkv_call(
        place, own, other, table, gain_attn.reshape(8, HD), gain_heads, docs
    )
    mixed, gu_columns, far_down, low_down = tie(mixed, gu_columns, far_down, low_down)

    got = all_to_all(mixed.reshape(8, 256, HD), CHIPS)

    own_gu = jnp.where(zero_core, gu_columns[:, 0], gu_columns[:, 1])
    other_gu = swap_core(jnp.where(zero_core, gu_columns[:, 1], gu_columns[:, 0]))
    gu, gu_gain = place_call(place, own_gu, other_gu, gain_mlp.reshape(8, HD))
    got, gu, gu_gain = tie(got, gu, gu_gain)

    keep, send = collect_call(place, got, sides_o)
    middle = x + keep + swap_core(send).astype(F32)
    unit_two, factor_two = normalize(middle)
    unit_two_low, w_back, far_down = tie(unit_two.astype(BF), w_back, far_down)

    down = by_xhi(low_down, far_down)
    dy_own = back_by_y(dy_own).reshape(512, D)
    dy_other = swap_core(dy_own)
    inner_grad_own = mm_nt(dy_own, down)
    inner_grad_other = mm_nt(dy_other, down)
    tokens_own = jnp.concatenate(
        [unit_two_low] + [shift_y(unit_two_low, r) for r in range(1, 4)], axis=0
    )
    tokens_own, mixed, w_far, inner_grad_own, inner_grad_other = tie(
        tokens_own, mixed, swap_x(w_back), inner_grad_own, inner_grad_other
    )
    halves = mixed.reshape(2, 1024, HD)
    mixed_keep = jnp.where(zero_xhi, halves[0], halves[1])
    mixed_send = jnp.where(zero_xhi, halves[1], halves[0])
    tokens_other = swap_core(tokens_own)
    part, inner, grad_gu = mlp_call(
        tokens_own, tokens_other, inner_grad_own, inner_grad_other, gu_gain
    )
    part = (part[:512].astype(F32) + swap_core(part[512:]).astype(F32)).astype(BF)

    part, mixed_send, tokens_own, tokens_other, inner, grad_gu = tie(
        part, mixed_send, tokens_own, tokens_other, inner, grad_gu
    )
    shifted = [shift_y(part[128 * r : 128 * r + 128], -r) for r in range(1, 4)]
    sum_gu, gain_mlp_grad = grad_columns_call(
        place, (tokens_own, tokens_other), (grad_gu,), gain_mlp.reshape(8, HD), gu
    )
    sum_down = grad_rows_call((inner,), (dy_own, dy_other))
    packet = jnp.concatenate([sum_gu.reshape(8, 384, 256), sum_down.reshape(8, 192, 256)], axis=1)
    *shifted, packet, mixed_got = tie(*shifted, packet, swap_xhi(mixed_send))
    packet = lax.psum_scatter(packet.reshape(8 * 576, 256), DP, scatter_dimension=0, tiled=True)
    grad_unit_two = part[:128].astype(F32)
    for value in shifted:
        grad_unit_two += value.astype(F32)
    grad_middle = grad_out.astype(F32) + norm_back(grad_unit_two, unit_two, factor_two)
    grad_middle_low = grad_middle.astype(BF)
    grad_middle_half = lax.all_gather(grad_middle_low, YC, axis=0, tiled=True)
    blocks = to_heads_call(place, grad_middle_low, swap_core(grad_middle_low), sides_o)
    blocks, mixed_keep, mixed_got, inner = tie(blocks, mixed_keep, mixed_got, inner)
    grad_mixed = all_to_all(blocks, CHIPS).reshape(SEQLEN, HD)
    mixed_pair = by_xhi(mixed_keep, mixed_got, axis=1)
    out_part = mm(inner[:512], down) + swap_core(mm(inner[512:], down).astype(BF)).astype(F32)
    out_part = out_part.astype(BF)
    out_part = back_by_y(out_part.reshape(4, 128, D)).reshape(512, D)
    grad_mixed, mixed_pair, out_part = tie(grad_mixed, mixed_pair, out_part)

    dq, keep, send, gain_part = attend_back_call(
        place, q, qx, k, kx, v, mixed, total, gain_heads, grad_mixed, raw, table
    )
    dq, keep, send, packet = tie(dq, keep, send, packet)

    near, far = join_call(place, dq, keep, swap_core(send))
    near, far, packet = tie(near, far, packet)
    parts_gu = all_to_all(packet[:384].reshape(16, 24, 256), SEQ)
    rows_down = packet[384:].reshape(4, 2, 24, 256)
    kept = jnp.where(zero_xhi, rows_down[:, 0], rows_down[:, 1]).astype(F32)
    came = swap_xhi(jnp.where(zero_xhi, rows_down[:, 1], rows_down[:, 0]))
    sum_heads, gain_attn_grad = grad_columns_call(
        place, (unit_all,), (near, far), gain_attn.reshape(8, HD), w_mine
    )
    far = swap_xhi(far)
    sum_heads, mixed_pair = tie(sum_heads, mixed_pair)
    sum_o = grad_rows_call((mixed_pair,), (grad_middle_half,))
    sum_gains = jnp.concatenate(
        [gain_attn_grad[:, 0], gain_mlp_grad[:, 0], gain_part[0], gain_part[1]]
    ).astype(BF)
    sum_gains = jnp.pad(sum_gains.reshape(9, 256), ((0, 7), (0, 0)))
    sums = jnp.concatenate(
        [
            sum_heads.reshape(8, 128, 256),
            sum_o.reshape(8, 128, 256),
            jnp.broadcast_to(sum_gains[None], (8, 16, 256)),
        ],
        axis=1,
    )
    sums, parts_gu, came, far = tie(sums, parts_gu, came, far)
    sums = all_to_all(sums, DP)
    rows_gu = rows_call(parts_gu)
    rows_down = (kept + came.astype(F32)).transpose(1, 0, 2).reshape(24, D)
    wide = jnp.concatenate([rows_gu, rows_down.reshape(8, 3 * D)], axis=1).astype(BF)
    near, far, wide = tie(near, far, wide)
    wide = lax.all_gather(wide, DP, axis=0, tiled=True)
    mine, theirs = back_call(place, near, far, w_back, w_far)
    sums, mine, theirs, out_part = tie(sums, mine, theirs, out_part)
    output = lax.psum_scatter(out_part, "y", scatter_dimension=0, tiled=True)
    output = middle + output.astype(F32)
    sums = sums.astype(F32).sum(axis=0).astype(BF)
    sum_gains = jnp.pad(sums[256:265].reshape(16, 1, 144), ((0, 0), (0, 7), (0, 112)))
    parts = jnp.concatenate([sums[:128].reshape(16, 8, 256), sum_gains], axis=1)
    rows_o = sums[128:256].reshape(4, 2, 16, 256)
    parts = all_to_all(parts, SEQ)
    blocks = merge_call(place, mine, swap_core(theirs))
    parts, *blocks = tie(parts, *blocks)
    blocks = [blocks[0]] + [shift_y(blocks[n], n) for n in range(1, 4)]
    kept = jnp.where(zero_xhi, rows_o[:, 0], rows_o[:, 1]).astype(F32)
    came = swap_xhi(jnp.where(zero_xhi, rows_o[:, 1], rows_o[:, 0])).astype(F32)
    rows_o = (kept + came).transpose(1, 0, 2).reshape(16, D).astype(BF)
    grad_gains = parts[:, 8, :144].astype(F32).sum(axis=0)
    pick = lambda block: block.transpose(1, 0, 2).reshape(8, -1)
    pairs = parts[:, :8, HD:].reshape(8, 2, 8, HD)
    rows_qkv = jnp.concatenate(
        [pick(parts[:, :8, :HD]), pick(pairs[:, 0]), pick(pairs[:, 1])], axis=1
    )

    last = jnp.concatenate(
        [rows_qkv.reshape(8, 4, D).transpose(1, 0, 2).reshape(32, D), rows_o], axis=0
    )
    last = spread(last, DP, 8)
    updates = {}
    for index, grad in ((1, wide[:, : 2 * FF]), (3, wide[:, 2 * FF :].reshape(192, D))):
        updates[index] = adam(
            masters[index], grad.astype(F32), firsts[index], seconds[index], rates[index], DECAY
        )
    last, updates[1], updates[3] = tie(last, updates[1], updates[3])
    owned_qkv = last[:, :32].reshape(8, 4, 8, D).transpose(0, 2, 1, 3).reshape(64, 4096)
    owned_o = last[:, 32:].reshape(128, D)
    for index, grad, decay in ((0, owned_qkv, DECAY), (2, owned_o, DECAY), (4, grad_gains, 0.0)):
        updates[index] = adam(
            masters[index], grad.astype(F32), firsts[index], seconds[index], rates[index], decay
        )
    updates[0], updates[2], *blocks = tie(updates[0], updates[2], *blocks)
    total_back = blocks[0].astype(F32)
    for value in blocks[1:]:
        total_back += value.astype(F32)
    hidden_grad = grad_middle + norm_back(total_back, unit_one, factor_one)
    results = [output.astype(BF)[None], hidden_grad[None]]
    for index in range(5):
        results.extend(updates[index])
    return tuple(results)


def solution(mesh):
    fine = Mesh(mesh.devices.reshape(2, 4, 2, 4, 2), ("xlo", "z", "xhi", "y", "core"))
    tokens = P(DP, SEQ, None)
    rows = P(SEQ, None)
    return jax.shard_map(
        on_device,
        mesh=fine,
        in_specs=(tokens, tokens, P(DP, SEQ))
        + (rows, rows, rows, rows, P(SEQ)) * 3,
        out_specs=(tokens, tokens) + (rows,) * 12 + (P(SEQ),) * 3,
        check_vma=False,
    )
```

```python
import functools
import math

import jax
import jax.numpy as jnp
import numpy as np
from jax import lax
from jax.experimental import pallas as pl
from jax.experimental.pallas import tpu as pltpu
from jax.sharding import Mesh
from jax.sharding import PartitionSpec as P

D = 1024
H = 16
KVH = 8
HD = 128
FF = 3072
KEYS_SEEN = 512
STEP = 10
SEQLEN = 2048
EPSILON = 1e-06
THETA = 1000000.0
BETA_ONE = 0.9
BETA_TWO = 0.95
ADAM_EPSILON = 1e-08
DECAY = 0.1
STEP_SCALE = 1.5
GAIN_RATE = 0.8

SCALE = HD**-0.5
LOG2E = math.log2(math.e)
FAR = 1024.0
BLK = 512

DP = ("xlo", "z")
SEQ = ("xhi", "y", "core")
CHIPS = ("xhi", "y")
YC = ("y", "core")
ALL = DP + SEQ
MIB = 1024 * 1024
BF = jnp.bfloat16
F32 = jnp.float32


def mm(a, b):
    return jnp.dot(a, b, preferred_element_type=F32)


def mm_nt(a, b):
    return lax.dot_general(a, b, (((1,), (1,)), ((), ())), preferred_element_type=F32)


def mm_tn(a, b):
    return lax.dot_general(a, b, (((0,), (0,)), ((), ())), preferred_element_type=F32)


def normalize(value):
    factor = lax.rsqrt(jnp.mean(value * value, axis=-1, keepdims=True) + EPSILON)
    return value * factor, factor


def norm_back(grad_unit, unit, factor):
    return factor * (grad_unit - unit * jnp.mean(grad_unit * unit, axis=-1, keepdims=True))


def rope_table():
    freq = np.float32(THETA) ** (-np.arange(0, HD, 2).astype(np.float32) / np.float32(HD))
    angle = np.arange(SEQLEN, dtype=np.float32)[:, None] * freq.astype(np.float32)[None, :]
    return np.concatenate([np.cos(angle), np.sin(angle)], 1).astype(np.float32)


def swap_core(value):
    return lax.ppermute(value, "core", [(0, 1), (1, 0)])


def swap_x(value):
    return lax.ppermute(value, ("xlo", "xhi"), [(0, 3), (3, 0), (1, 2), (2, 1)])


def swap_xhi(value):
    return lax.ppermute(value, "xhi", [(0, 1), (1, 0)])


def all_to_all(value, axes):
    return lax.all_to_all(value, axes, split_axis=0, concat_axis=0, tiled=True)


def shift_y(value, by):
    return lax.ppermute(value, "y", [(n, (n + by) % 4) for n in range(4)])


def shift_chips(value, dx, dy):
    pairs = [(4 * a + b, 4 * (a ^ dx) + (b + dy) % 4) for a in range(2) for b in range(4)]
    return lax.ppermute(value, CHIPS, pairs)


def tie(*values):
    return lax.optimization_barrier(values)


def spread(value, axes, count):
    return all_to_all(jnp.broadcast_to(value[None], (count, *value.shape)), axes)


def cost(us):
    return pl.CostEstimate(
        flops=int(us * 1.1e9), bytes_accessed=int(us * 2e6), transcendentals=0
    )


SCALARS = pl.BlockSpec(memory_space=pltpu.SMEM)
WHOLE = pl.BlockSpec(memory_space=pltpu.VMEM)


def gather_weights(place, own, other, gain, w, mine_out, back_out):
    first = place[1] == 0
    columns = jnp.transpose(gain[...])
    for p in range(8):
        for c in range(2):
            block = jnp.where(first == (c == 0), own[p], other[p])
            for half in range(2):
                start = (2 * p + c) * 64 + half * 32
                rows = pl.ds(start, 32)
                at = half * 512
                query = jnp.where(first, block[:, at : at + HD], block[:, at + HD : at + 2 * HD])
                key = block[:, at + 2 * HD : at + 3 * HD]
                value = block[:, at + 3 * HD : at + 4 * HD]
                column = columns[start % 128 : start % 128 + 32, start // 128 : start // 128 + 1]
                heads = jnp.concatenate([query, key, value], axis=1).astype(F32) * column
                w[rows, :] = heads.astype(BF)
                mine = jnp.concatenate([query, jnp.where(first, key, value)], axis=1)
                mine_out[rows, :] = mine
                back_out[rows, :] = (mine.astype(F32) * column).astype(BF)


def document_columns(docs, qx, kx):
    columns = jnp.transpose(docs[...])
    lane = lax.broadcasted_iota(jnp.int32, (128, HD), 1)
    for n in range(16):
        rows = pl.ds(128 * n, 128)
        same = columns[:, n : n + 1] == lane.astype(F32)
        qx[rows, :] = jnp.where(same & (lane < 8), -FAR, 0.0).astype(BF)
        kx[rows, :] = jnp.where(same | (lane >= 16), 0.0, 1.0).astype(BF)


def qkv_kernel(
    place, own, other, own_w, other_w, table, gain, gains, docs,
    x_out, q_out, k_out, v_out, raw_out, out, total, qx, kx, mine_out, back_out, q, k, v, w,
):
    step = pl.program_id(0)
    first = place[1] == 0

    @pl.when(step == 0)
    def _():
        gather_weights(place, own_w, other_w, gain, w, mine_out, back_out)
        document_columns(docs, qx, kx)

    x = []
    for n in range(2):
        a, b = own[n], other[n]
        x += [jnp.where(first, a, b), jnp.where(first, b, a)]
    x = jnp.concatenate(x, axis=0)
    x_out[...] = x
    qkv = mm(x, w[...])
    raw_out[...] = qkv[:, : 2 * HD]
    cos, sin = unpack_table(table[...])
    rows = pl.ds(pl.multiple_of(step * 512, 512), 512)

    def rotated(part, gain):
        unit, _ = normalize(part)
        value = unit * gain
        return value * cos + pltpu.roll(value, HD // 2, 1) * sin

    query = (rotated(qkv[:, :HD], gains[0:1, :]) * (SCALE * LOG2E)).astype(BF)
    key = rotated(qkv[:, HD : 2 * HD], gains[1:2, :]).astype(BF)
    value = qkv[:, 2 * HD :].astype(BF)
    q_out[...] = query
    k_out[...] = key
    v_out[...] = value
    q[rows, :] = query
    k[rows, :] = key
    v[rows, :] = value

    @pl.when(step == SEQLEN // 512 - 1)
    def _():
        attend(q, qx, k, kx, v, out, total)


def attend(q, qx, k, kx, v, out, total):
    ones = jnp.ones((BLK, HD), BF)
    causal = lax.broadcasted_iota(jnp.int32, (BLK, BLK), 1) <= lax.broadcasted_iota(
        jnp.int32, (BLK, BLK), 0
    )
    for i in range(SEQLEN // BLK):
        rows = pl.ds(i * BLK, BLK)
        query = jnp.concatenate([q[rows, :], qx[rows, :]], axis=1)
        acc = None
        for j in range(i + 1):
            cols = pl.ds(j * BLK, BLK)
            key = jnp.concatenate([k[cols, :], kx[cols, :]], axis=1)
            prob = jnp.exp2(mm_nt(query, key))
            if i == j:
                prob = jnp.where(causal, prob, 0.0)
            term = mm(prob.astype(BF), jnp.concatenate([v[cols, :], ones], axis=1))
            acc = term if acc is None else acc + term
        total[rows, :] = acc[:, HD:]
        out[rows, :] = (acc[:, :HD] / acc[:, HD:]).astype(BF)


def unpack_table(table):
    low = lax.broadcasted_iota(jnp.int32, table.shape, 1) < HD // 2
    turned = pltpu.roll(table, HD // 2, 1)
    return jnp.where(low, table, turned), jnp.where(low, -turned, table)


def qkv_call(place, own, other, table, gain, gains, docs):
    rows = 512
    part = pl.BlockSpec((2, 128, D), lambda p, c: (p, 0, 0))
    weights = pl.BlockSpec((8, 32, D), lambda p, c: (0, 4, 0))
    whole = lambda shape: pl.BlockSpec(shape, lambda p, c: (0, 0))
    tokens = lambda width: pl.BlockSpec((rows, width), lambda p, c: (p, 0))
    heads = jax.ShapeDtypeStruct((SEQLEN, HD), BF)
    columns = jax.ShapeDtypeStruct((D, 256), BF)
    return pl.pallas_call(
        qkv_kernel,
        grid_spec=pltpu.PrefetchScalarGridSpec(
            num_scalar_prefetch=1,
            grid=(SEQLEN // rows,),
            in_specs=[part, part, weights, weights, tokens(HD)]
            + [whole((8, HD)), whole((8, HD)), whole((16, HD))],
            out_specs=[tokens(D), tokens(HD), tokens(HD), tokens(HD), tokens(2 * HD)]
            + [whole((SEQLEN, HD))] * 4
            + [whole((D, 256))] * 2,
            scratch_shapes=[pltpu.VMEM((SEQLEN, HD), BF)] * 3 + [pltpu.VMEM((D, 384), BF)],
        ),
        out_shape=[
            jax.ShapeDtypeStruct((SEQLEN, D), BF),
            heads,
            heads,
            heads,
            jax.ShapeDtypeStruct((SEQLEN, 2 * HD), F32),
            heads,
            jax.ShapeDtypeStruct((SEQLEN, HD), F32),
            heads,
            heads,
            columns,
            columns,
        ],
        compiler_params=pltpu.CompilerParams(vmem_limit_bytes=58 * MIB),
        cost_estimate=cost(14),
        name="qkv_attend",
    )(place, own, other, own, other, table, gain, gains, docs)


def thirds(value):
    high = value.astype(BF).astype(F32)
    middle = (value - high).astype(BF).astype(F32)
    return high, middle, value - high - middle


def attend_back_kernel(
    place, q, qx, k, kx, v, out, total, gains, grad, raw_hbm, table_hbm,
    dq_out, keep_out, send_out, gain_out, qx_s, gx_s, dq_s, raw, table, sems,
):
    first = place[1] == 0
    late = [
        pltpu.make_async_copy(a, b, sems.at[n])
        for n, (a, b) in enumerate(((raw_hbm, raw), (table_hbm, table)))
    ]
    for copy in late:
        copy.start()
    count = SEQLEN // BLK
    lane = lax.broadcasted_iota(jnp.int32, (BLK, HD), 1)
    ones = jnp.ones((BLK, HD), BF)
    causal = lax.broadcasted_iota(jnp.int32, (BLK, BLK), 0) <= lax.broadcasted_iota(
        jnp.int32, (BLK, BLK), 1
    )

    def placed(parts, start):
        value = jnp.zeros((BLK, HD), F32)
        for n, part in enumerate(parts):
            value = jnp.where(lane == start + n, part, value)
        return value

    for i in range(count):
        rows = pl.ds(i * BLK, BLK)
        level = placed(thirds(jnp.log2(total[rows, :])), 8)
        qx_s[rows, :] = (qx[rows, :].astype(F32) - level).astype(BF)
        delta = jnp.sum(grad[rows, :].astype(F32) * out[rows, :].astype(F32), 1, keepdims=True)
        gx_s[rows, :] = (-placed(thirds(delta), 0)).astype(BF)

    def back(value, part, gain, rows):
        cos, sin = unpack_table(table[rows, :])
        turned = value * cos - pltpu.roll(value, HD // 2, 1) * sin
        unit, factor = normalize(raw[rows, pl.ds(part * HD, HD)])
        return (
            norm_back(turned * gain, unit, factor),
            jnp.sum(turned * unit, axis=0, keepdims=True),
        )

    gain_q = jnp.zeros((1, HD), F32)
    gain_k = jnp.zeros((1, HD), F32)
    for j in range(count):
        cols = pl.ds(j * BLK, BLK)
        key = jnp.concatenate([k[cols, :], kx[cols, :]], axis=1)
        value = jnp.concatenate([v[cols, :], ones], axis=1)
        dk = dv = None
        for i in range(j, count):
            rows = pl.ds(i * BLK, BLK)
            query = jnp.concatenate([q[rows, :], qx_s[rows, :]], axis=1)
            given = jnp.concatenate([grad[rows, :], gx_s[rows, :]], axis=1)
            prob = jnp.exp2(mm_nt(key, query))
            if i == j:
                prob = jnp.where(causal, prob, 0.0)
            score = (prob * mm_nt(value, given)).astype(BF)
            dv_term = mm(prob.astype(BF), grad[rows, :])
            dk_term = mm(score, q[rows, :])
            dq_term = mm_tn(score, k[cols, :])
            dv = dv_term if dv is None else dv + dv_term
            dk = dk_term if dk is None else dk + dk_term
            if j == 0:
                dq_s[rows, :] = dq_term
            else:
                dq_s[rows, :] += dq_term
        if j == 0:
            for copy in late:
                copy.wait()
        dk, gain = back(dk * (1.0 / LOG2E), 1, gains[1:2, :], cols)
        keep_out[cols, :] = jnp.where(first, dk, dv).astype(BF)
        send_out[cols, :] = jnp.where(first, dv, dk).astype(BF)
        gain_k += gain
        dq, gain = back(dq_s[cols, :] * SCALE, 0, gains[0:1, :], cols)
        dq_out[cols, :] = dq.astype(BF)
        gain_q += gain
    gain_out[...] = jnp.concatenate([gain_q, gain_k, jnp.zeros((6, HD), F32)], axis=0)


def attend_back_call(*args):
    tokens = jax.ShapeDtypeStruct((SEQLEN, HD), BF)
    return pl.pallas_call(
        attend_back_kernel,
        out_shape=[tokens, tokens, tokens, jax.ShapeDtypeStruct((8, HD), F32)],
        in_specs=[SCALARS]
        + [WHOLE] * (len(args) - 3)
        + [pl.BlockSpec(memory_space=pl.ANY)] * 2,
        scratch_shapes=[
            pltpu.VMEM((SEQLEN, HD), BF),
            pltpu.VMEM((SEQLEN, HD), BF),
            pltpu.VMEM((SEQLEN, HD), F32),
            pltpu.VMEM((SEQLEN, 2 * HD), F32),
            pltpu.VMEM((SEQLEN, HD), F32),
            pltpu.SemaphoreType.DMA((2,)),
        ],
        compiler_params=pltpu.CompilerParams(vmem_limit_bytes=58 * MIB),
        cost_estimate=cost(12),
        name="attend_back",
    )(*args)


def columns_kernel(w, out):
    for n in range(8):
        for g in range(4):
            part = w[:, pl.ds(192 * (8 * g + n), 192)].astype(BF)
            out[n // 2, n % 2, :, pl.ds(192 * g, 192)] = part
            out[4 + n // 2, n % 2, :, pl.ds(192 * g, 192)] = part


def columns_call(w):
    return pl.pallas_call(
        columns_kernel,
        out_shape=jax.ShapeDtypeStruct((8, 2, 64, 768), BF),
        compiler_params=pltpu.CompilerParams(vmem_limit_bytes=16 * MIB),
        cost_estimate=cost(1),
        name="columns",
    )(w)


def place_kernel(place, own, other, gain, raw_out, gained_out):
    columns = jnp.transpose(gain[...])
    first = place[1] == 0
    for p in range(8):
        for c in range(2):
            rows = pl.ds((2 * p + c) * 64, 64)
            block = jnp.where(first == (c == 0), own[p], other[p])
            raw_out[rows, :] = block
            column = columns[64 * c : 64 * c + 64, p : p + 1]
            gained_out[rows, :] = (block.astype(F32) * column).astype(BF)


def place_call(place, own, other, gain):
    return pl.pallas_call(
        place_kernel,
        out_shape=[jax.ShapeDtypeStruct((D, 768), BF)] * 2,
        in_specs=[SCALARS, WHOLE, WHOLE, WHOLE],
        compiler_params=pltpu.CompilerParams(vmem_limit_bytes=24 * MIB),
        cost_estimate=cost(1.5),
        name="place",
    )(place, own, other, gain)


def collect_kernel(place, got, w, keep_out, send_out):
    def rows_of(c):
        rows = pl.ds(pl.multiple_of(c * 128, 128), 128)
        left = jnp.concatenate([got[n, rows, :] for n in range(8)], axis=1)
        right = jnp.concatenate([w[quarter, n] for n in range(8) for quarter in range(4)], axis=0)
        return mm(left, right)

    send_out[...] = rows_of(1 - place[1]).astype(BF)
    keep_out[...] = rows_of(place[1])


def collect_call(place, got, w):
    return pl.pallas_call(
        collect_kernel,
        out_shape=[jax.ShapeDtypeStruct((128, D), F32), jax.ShapeDtypeStruct((128, D), BF)],
        in_specs=[SCALARS, WHOLE, WHOLE],
        compiler_params=pltpu.CompilerParams(vmem_limit_bytes=32 * MIB),
        cost_estimate=cost(2),
        name="collect",
    )(place, got, w)


def to_heads_kernel(place, mine, others, w, out):
    core = place[1]
    for c, value in ((core, mine), (1 - core, others)):
        rows = pl.ds(pl.multiple_of(c * 128, 128), 128)
        for n in range(8):
            right = jnp.concatenate([w[quarter, n] for quarter in range(4)], axis=0)
            out[n, rows, :] = mm_nt(value[...], right).astype(BF)


def to_heads_call(*args):
    return pl.pallas_call(
        to_heads_kernel,
        out_shape=jax.ShapeDtypeStruct((8, 256, HD), BF),
        in_specs=[SCALARS] + [WHOLE] * 3,
        compiler_params=pltpu.CompilerParams(vmem_limit_bytes=16 * MIB),
        cost_estimate=cost(2),
        name="to_heads",
    )(*args)


def join_kernel(place, query, keep, got, near_out, far_out):
    for side, out in ((place[0], near_out), (1 - place[0], far_out)):
        rows = pl.ds(pl.multiple_of(side * 1024, 1024), 1024)
        total = keep[rows, :].astype(F32) + got[rows, :].astype(F32)
        out[...] = jnp.concatenate([query[rows, :], total.astype(BF)], axis=1)


def join_call(*args):
    half = jax.ShapeDtypeStruct((1024, 256), BF)
    return pl.pallas_call(
        join_kernel,
        out_shape=[half, half],
        in_specs=[SCALARS] + [WHOLE] * 3,
        compiler_params=pltpu.CompilerParams(vmem_limit_bytes=24 * MIB),
        cost_estimate=cost(1.5),
        name="join",
    )(*args)


def back_kernel(place, near, far, w_near, w_far, keep_out, send_out):
    first = place[1] == 0
    part = mm_nt(near[...], w_near[...]) + mm_nt(far[...], w_far[...])
    part = part.astype(BF)
    keep_out[0] = jnp.where(first, part[:128], part[128:])
    send_out[0] = jnp.where(first, part[128:], part[:128])


def back_call(place, near, far, w_near, w_far):
    tokens = pl.BlockSpec((256, 256), lambda p, c: (p, 0))
    whole = pl.BlockSpec((D, 256), lambda p, c: (0, 0))
    chip = pl.BlockSpec((1, 128, D), lambda p, c: (p, 0, 0))
    return pl.pallas_call(
        back_kernel,
        grid_spec=pltpu.PrefetchScalarGridSpec(
            num_scalar_prefetch=1,
            grid=(4,),
            in_specs=[tokens, tokens, whole, whole],
            out_specs=[chip, chip],
        ),
        out_shape=[jax.ShapeDtypeStruct((4, 128, D), BF)] * 2,
        compiler_params=pltpu.CompilerParams(vmem_limit_bytes=24 * MIB),
        cost_estimate=cost(3),
        name="back",
    )(place, near, far, w_near, w_far)


def merge_kernel(place, keep, got, *outs):
    for dy in range(4):
        n = lax.rem(place[2] + dy, 4)
        outs[dy][...] = (keep[n].astype(F32) + got[n].astype(F32)).astype(BF)


def merge_call(*args):
    return pl.pallas_call(
        merge_kernel,
        out_shape=[jax.ShapeDtypeStruct((128, D), BF)] * 4,
        in_specs=[SCALARS] + [WHOLE] * 2,
        compiler_params=pltpu.CompilerParams(vmem_limit_bytes=24 * MIB),
        cost_estimate=cost(1),
        name="merge",
    )(*args)


def mlp_kernel(own, other, own_given, other_given, w, part_out, inner_out, grad_out):
    mine = pl.program_id(0) < 2
    x = jnp.where(mine, own[...], other[...])
    given = jnp.where(mine, own_given[...], other_given[...])
    gate_up = mm(x, w[...])
    gate, up = gate_up[:, :384], gate_up[:, 384:]
    sigmoid = jax.nn.sigmoid(gate)
    silu = gate * sigmoid
    inner_out[...] = (silu * up).astype(BF)
    grad_gate = given * up * sigmoid * (1.0 + gate * (1.0 - sigmoid))
    grad = jnp.concatenate([grad_gate, given * silu], axis=1).astype(BF)
    grad_out[...] = grad
    part_out[...] = mm_nt(grad, w[...]).astype(BF)


def mlp_call(own, other, own_given, other_given, w):
    rows = 256
    first = lambda width: pl.BlockSpec((rows, width), lambda i: (jnp.minimum(i, 1), 0))
    second = lambda width: pl.BlockSpec((rows, width), lambda i: (jnp.maximum(i - 2, 0), 0))
    tokens = lambda width: pl.BlockSpec((rows, width), lambda i: (i, 0))
    return pl.pallas_call(
        mlp_kernel,
        grid=(1024 // rows,),
        in_specs=[first(D), second(D), first(384), second(384)]
        + [pl.BlockSpec((D, 768), lambda i: (0, 0))],
        out_specs=[tokens(D), tokens(384), tokens(768)],
        out_shape=[
            jax.ShapeDtypeStruct((1024, D), BF),
            jax.ShapeDtypeStruct((1024, 384), BF),
            jax.ShapeDtypeStruct((1024, 768), BF),
        ],
        compiler_params=pltpu.CompilerParams(vmem_limit_bytes=24 * MIB),
        cost_estimate=cost(6.2),
        name="mlp",
    )(own, other, own_given, other_given, w)


def product_of_halves(place, x, near, far):
    total = None
    for side, d in ((place[0], near), (1 - place[0], far)):
        rows = pl.ds(pl.multiple_of(side * 1024, 1024), 1024)
        term = mm_tn(x[rows, :], d[...])
        total = term if total is None else total + term
    return total


def product_of_parts(xs, ds):
    total, start = None, 0
    for n in range(max(len(xs), len(ds))):
        x, d = xs[min(n, len(xs) - 1)], ds[min(n, len(ds) - 1)]
        rows = min(x.shape[0], d.shape[0])
        x = x[pl.ds(start, rows), :] if x.shape[0] > rows else x[...]
        d = d[pl.ds(start, rows), :] if d.shape[0] > rows else d[...]
        term = mm_tn(x, d)
        total = term if total is None else total + term
        start += rows
    return total


def grad_columns_kernel(counts, place, *refs):
    a, b = counts
    gain, w, out, gain_out = refs[a + b :]
    if a == 1:
        total = product_of_halves(place, refs[0], refs[1], refs[2])
    else:
        total = product_of_parts(refs[:a], refs[a : a + b])
    gain_out[...] = jnp.sum(total * w[...].astype(F32), axis=1, keepdims=True)
    columns = jnp.transpose(gain[...])
    lane = lax.broadcasted_iota(jnp.int32, columns.shape, 1) - 2 * pl.program_id(0)
    pick = lambda n: jnp.sum(jnp.where(lane == n, columns, 0.0), axis=1, keepdims=True)
    total = total * jnp.concatenate([pick(0), pick(1)], axis=0)
    for q in range(8):
        for j in range(4):
            piece = total[64 * j + 8 * q : 64 * j + 8 * q + 8]
            groups = [piece[:, g : g + 256] for g in range(0, piece.shape[1], 256)]
            out[q, j] = jnp.concatenate(groups, axis=0).astype(BF)


def grad_columns_call(place, xs, ds, gain, w):
    width = w.shape[1]
    return pl.pallas_call(
        functools.partial(grad_columns_kernel, (len(xs), len(ds))),
        grid_spec=pltpu.PrefetchScalarGridSpec(
            num_scalar_prefetch=1,
            grid=(4,),
            in_specs=[pl.BlockSpec((x.shape[0], 256), lambda t, c: (0, t)) for x in xs]
            + [pl.BlockSpec(d.shape, lambda t, c: (0, 0)) for d in ds]
            + [pl.BlockSpec((8, HD), lambda t, c: (0, 0))]
            + [pl.BlockSpec((256, width), lambda t, c: (t, 0))],
            out_specs=[
                pl.BlockSpec((8, 4, width // 32, 256), lambda t, c: (0, t, 0, 0)),
                pl.BlockSpec((256, 1), lambda t, c: (t, 0)),
            ],
        ),
        out_shape=[
            jax.ShapeDtypeStruct((8, 16, width // 32, 256), BF),
            jax.ShapeDtypeStruct((D, 1), F32),
        ],
        compiler_params=pltpu.CompilerParams(vmem_limit_bytes=24 * MIB),
        cost_estimate=cost(3.4),
        name="grad_columns",
    )(place, *xs, *ds, gain, w)


def rows_kernel(got, out):
    for n in range(8):
        total = got[n].astype(F32) + got[8 + n].astype(F32)
        total = jnp.concatenate([total[0:8], total[8:16], total[16:24]], axis=1)
        for g in range(4):
            out[:, pl.ds(192 * (8 * g + n), 192)] = total[:, 192 * g : 192 * g + 192]


def rows_call(got):
    return pl.pallas_call(
        rows_kernel,
        out_shape=jax.ShapeDtypeStruct((8, 2 * FF), F32),
        compiler_params=pltpu.CompilerParams(vmem_limit_bytes=16 * MIB),
        cost_estimate=cost(1),
        name="rows",
    )(got)


def grad_rows_kernel(counts, *refs):
    a, b = counts
    out = refs[a + b]
    step = out.shape[2] // 2
    total = product_of_parts(refs[:a], refs[a : a + b])
    for q in range(8):
        low, high = q * step, (8 + q) * step
        piece = jnp.concatenate([total[low : low + step], total[high : high + step]], axis=0)
        out[q, 0] = piece.astype(BF)


def grad_rows_call(xs, ds):
    rows = xs[0].shape[1] // 8
    return pl.pallas_call(
        functools.partial(grad_rows_kernel, (len(xs), len(ds))),
        grid=(4,),
        in_specs=[pl.BlockSpec(x.shape, lambda t: (0, 0)) for x in xs]
        + [pl.BlockSpec((d.shape[0], 256), lambda t: (0, t)) for d in ds],
        out_specs=pl.BlockSpec((8, 1, rows, 256), lambda t: (0, t, 0, 0)),
        out_shape=jax.ShapeDtypeStruct((8, 4, rows, 256), BF),
        compiler_params=pltpu.CompilerParams(vmem_limit_bytes=24 * MIB),
        cost_estimate=cost(3),
        name="grad_rows",
    )(*xs, *ds)


def adam(weight, grad, first, second, rate, decay):
    first = BETA_ONE * first + (1.0 - BETA_ONE) * grad
    second = BETA_TWO * second + (1.0 - BETA_TWO) * grad * grad
    ratio = (
        first / (1.0 - BETA_ONE**STEP) / (jnp.sqrt(second / (1.0 - BETA_TWO**STEP)) + ADAM_EPSILON)
    )
    return (first, second, weight - rate * (ratio + decay * weight))


def on_device(
    hidden, cotangent, segments, w_qkv, w_gu, w_o, w_down, norm_gains,
    m_qkv, m_gu, m_o, m_down, m_gains, v_qkv, v_gu, v_o, v_down, v_gains,
):
    core = lax.axis_index("core")
    xhi = lax.axis_index("xhi")
    zero_core = core == 0
    zero_xhi = xhi == 0
    y = lax.axis_index("y")
    z = lax.axis_index("z")
    place = jnp.stack([xhi, core, y]).astype(jnp.int32)

    def by_xhi(own, other, axis=0):
        return jnp.concatenate(
            [jnp.where(zero_xhi, own, other), jnp.where(zero_xhi, other, own)], axis=axis
        )

    def back_by_y(value):
        return jnp.concatenate(
            [lax.dynamic_slice_in_dim(value, (y + 4 - r) % 4, 1, 0) for r in range(4)], axis=0
        )

    masters = (w_qkv, w_gu, w_o, w_down, norm_gains)
    rates = (
        STEP_SCALE / math.sqrt(D),
        STEP_SCALE / math.sqrt(D),
        STEP_SCALE / math.sqrt(H * HD * 4 // KEYS_SEEN),
        STEP_SCALE / math.sqrt(FF),
        GAIN_RATE,
    )
    firsts = (m_qkv, m_gu, m_o, m_down, m_gains)
    seconds = (v_qkv, v_gu, v_o, v_down, v_gains)
    grad_out = cotangent[0]
    low_qkv, low_o, low_down = (w.astype(BF) for w in (w_qkv, w_o, w_down))

    x = hidden[0].astype(F32)
    unit_one, factor_one = normalize(x)
    columns = jnp.concatenate(
        [
            low_qkv[:, : H * HD].reshape(64, 8, 256),
            low_qkv[:, H * HD : (H + KVH) * HD].reshape(64, 8, HD),
            low_qkv[:, (H + KVH) * HD :].reshape(64, 8, HD),
        ],
        axis=-1,
    ).transpose(1, 0, 2)
    columns = jnp.concatenate([columns[:, :32], columns[:, 32:]], axis=-1)
    small = jnp.concatenate(
        [
            norm_gains.astype(BF),
            jnp.zeros((112,), BF),
            segments[0].astype(BF),
            jnp.zeros((640,), BF),
        ]
    )
    small = jnp.concatenate([small[None], jnp.zeros((15, D), BF)], axis=0)
    quarter_o = lax.dynamic_slice_in_dim(low_o, z * 32, 32, 0)
    spread_x = jnp.broadcast_to(unit_one.astype(BF)[None], (8, 128, D))
    same = jnp.concatenate([quarter_o, small], axis=0)
    same = jnp.broadcast_to(same[None], (8, 48, D))
    packet = jnp.concatenate([spread_x, columns, same], axis=1)
    own = all_to_all(packet, CHIPS)
    gu_columns = columns_call(w_gu)
    own, low_down, gu_columns = tie(own, low_down, gu_columns)
    other = swap_core(own)
    small = jnp.stack(
        [
            jnp.where(zero_core, own[:, 192], other[:, 192]),
            jnp.where(zero_core, other[:, 192], own[:, 192]),
        ],
        axis=1,
    ).reshape(16, D)
    gains = small[:, :144].reshape(2304).astype(F32)
    docs = small[:, 256:384].astype(F32)
    gain_attn, gain_mlp = gains[:D], gains[D : 2 * D]
    gain_heads = jnp.concatenate([gains[2 * D :].reshape(2, HD), jnp.zeros((6, HD), F32)], axis=0)
    table = jnp.asarray(rope_table())

    gu_columns = all_to_all(gu_columns, CHIPS)

    sides_o = lax.all_gather(own[:, 160:192], "z", axis=0, tiled=False)
    sides_o, dy_mine = tie(sides_o, grad_out)
    dy_own = lax.all_gather(dy_mine, "y", axis=0, tiled=False)
    unit_all, q, k, v, raw, mixed, total, qx, kx, w_mine, w_back = qkv_call(
        place, own, other, table, gain_attn.reshape(8, HD), gain_heads, docs
    )
    mixed, gu_columns, low_down = tie(mixed, gu_columns, low_down)

    got = all_to_all(mixed.reshape(8, 256, HD), CHIPS)

    own_gu = jnp.where(zero_core, gu_columns[:, 0], gu_columns[:, 1])
    other_gu = swap_core(jnp.where(zero_core, gu_columns[:, 1], gu_columns[:, 0]))
    gu, gu_gain = place_call(place, own_gu, other_gu, gain_mlp.reshape(8, HD))
    got, gu, gu_gain = tie(got, gu, gu_gain)

    keep, send = collect_call(place, got, sides_o)
    middle = x + keep + swap_core(send).astype(F32)
    unit_two, factor_two = normalize(middle)
    unit_two_low, w_back, low_down = tie(
        unit_two.astype(BF), w_back, low_down
    )
    far_down = swap_x(low_down)

    down = by_xhi(low_down, far_down)
    dy_own = back_by_y(dy_own).reshape(512, D)
    dy_other = swap_core(dy_own)
    inner_grad_own = mm_nt(dy_own, down)
    inner_grad_other = mm_nt(dy_other, down)
    tokens_own = jnp.concatenate(
        [unit_two_low] + [shift_y(unit_two_low, r) for r in range(1, 4)], axis=0
    )
    tokens_own, mixed, w_back, inner_grad_own, inner_grad_other = tie(
        tokens_own, mixed, w_back, inner_grad_own, inner_grad_other
    )
    halves = mixed.reshape(2, 1024, HD)
    mixed_keep = jnp.where(zero_xhi, halves[0], halves[1])
    mixed_send = jnp.where(zero_xhi, halves[1], halves[0])
    tokens_other = swap_core(tokens_own)
    part, inner, grad_gu = mlp_call(
        tokens_own, tokens_other, inner_grad_own, inner_grad_other, gu_gain
    )
    part = (part[:512].astype(F32) + swap_core(part[512:]).astype(F32)).astype(BF)

    part, mixed_send, tokens_own, tokens_other, inner, grad_gu = tie(
        part, mixed_send, tokens_own, tokens_other, inner, grad_gu
    )
    shifted = [shift_y(part[128 * r : 128 * r + 128], -r) for r in range(1, 4)]
    sum_gu, gain_mlp_grad = grad_columns_call(
        place, (tokens_own, tokens_other), (grad_gu,), gain_mlp.reshape(8, HD), gu
    )
    sum_down = grad_rows_call((inner,), (dy_own, dy_other))
    packet = jnp.concatenate([sum_gu.reshape(8, 384, 256), sum_down.reshape(8, 192, 256)], axis=1)
    *shifted, packet, mixed_got = tie(*shifted, packet, swap_xhi(mixed_send))
    packet = lax.psum_scatter(packet.reshape(8 * 576, 256), DP, scatter_dimension=0, tiled=True)
    grad_unit_two = part[:128].astype(F32)
    for value in shifted:
        grad_unit_two += value.astype(F32)
    grad_middle = grad_out.astype(F32) + norm_back(grad_unit_two, unit_two, factor_two)
    grad_middle_low = grad_middle.astype(BF)
    grad_middle_half = lax.all_gather(grad_middle_low, YC, axis=0, tiled=True)
    blocks = to_heads_call(place, grad_middle_low, swap_core(grad_middle_low), sides_o)
    blocks, mixed_keep, mixed_got, inner, w_far = tie(
        blocks, mixed_keep, mixed_got, inner, swap_x(w_back)
    )
    grad_mixed = all_to_all(blocks, CHIPS).reshape(SEQLEN, HD)
    mixed_pair = by_xhi(mixed_keep, mixed_got, axis=1)
    out_part = mm(inner[:512], down) + swap_core(mm(inner[512:], down).astype(BF)).astype(F32)
    out_part = out_part.astype(BF)
    out_part = back_by_y(out_part.reshape(4, 128, D)).reshape(512, D)
    grad_mixed, mixed_pair, out_part = tie(grad_mixed, mixed_pair, out_part)

    dq, keep, send, gain_part = attend_back_call(
        place, q, qx, k, kx, v, mixed, total, gain_heads, grad_mixed, raw, table
    )
    dq, keep, send, packet = tie(dq, keep, send, packet)

    near, far = join_call(place, dq, keep, swap_core(send))
    near, far, packet = tie(near, far, packet)
    parts_gu = all_to_all(packet[:384].reshape(16, 24, 256), SEQ)
    rows_down = packet[384:].reshape(4, 2, 24, 256)
    kept = jnp.where(zero_xhi, rows_down[:, 0], rows_down[:, 1]).astype(F32)
    came = swap_xhi(jnp.where(zero_xhi, rows_down[:, 1], rows_down[:, 0]))
    sum_heads, gain_attn_grad = grad_columns_call(
        place, (unit_all,), (near, far), gain_attn.reshape(8, HD), w_mine
    )
    far = swap_xhi(far)
    sum_heads, mixed_pair = tie(sum_heads, mixed_pair)
    sum_o = grad_rows_call((mixed_pair,), (grad_middle_half,))
    sum_gains = jnp.concatenate(
        [gain_attn_grad[:, 0], gain_mlp_grad[:, 0], gain_part[0], gain_part[1]]
    ).astype(BF)
    sum_gains = jnp.pad(sum_gains.reshape(9, 256), ((0, 7), (0, 0)))
    sums = jnp.concatenate(
        [
            sum_heads.reshape(8, 128, 256),
            sum_o.reshape(8, 128, 256),
            jnp.broadcast_to(sum_gains[None], (8, 16, 256)),
        ],
        axis=1,
    )
    sums, parts_gu, came, far = tie(sums, parts_gu, came, far)
    sums = all_to_all(sums, DP)
    rows_gu = rows_call(parts_gu)
    rows_down = (kept + came.astype(F32)).transpose(1, 0, 2).reshape(24, D)
    wide = jnp.concatenate([rows_gu, rows_down.reshape(8, 3 * D)], axis=1).astype(BF)
    near, far, wide = tie(near, far, wide)
    wide = lax.all_gather(wide, DP, axis=0, tiled=True)
    mine, theirs = back_call(place, near, far, w_back, w_far)
    sums, mine, theirs, out_part = tie(sums, mine, theirs, out_part)
    output = lax.psum_scatter(out_part, "y", scatter_dimension=0, tiled=True)
    output = middle + output.astype(F32)
    sums = sums.astype(F32).sum(axis=0).astype(BF)
    sum_gains = jnp.pad(sums[256:265].reshape(16, 1, 144), ((0, 0), (0, 7), (0, 112)))
    parts = jnp.concatenate([sums[:128].reshape(16, 8, 256), sum_gains], axis=1)
    rows_o = sums[128:256].reshape(4, 2, 16, 256)
    parts = all_to_all(parts, SEQ)
    blocks = merge_call(place, mine, swap_core(theirs))
    parts, *blocks = tie(parts, *blocks)
    blocks = [blocks[0]] + [shift_y(blocks[n], n) for n in range(1, 4)]
    kept = jnp.where(zero_xhi, rows_o[:, 0], rows_o[:, 1]).astype(F32)
    came = swap_xhi(jnp.where(zero_xhi, rows_o[:, 1], rows_o[:, 0])).astype(F32)
    rows_o = (kept + came).transpose(1, 0, 2).reshape(16, D).astype(BF)
    grad_gains = parts[:, 8, :144].astype(F32).sum(axis=0)
    pick = lambda block: block.transpose(1, 0, 2).reshape(8, -1)
    pairs = parts[:, :8, HD:].reshape(8, 2, 8, HD)
    rows_qkv = jnp.concatenate(
        [pick(parts[:, :8, :HD]), pick(pairs[:, 0]), pick(pairs[:, 1])], axis=1
    )

    last = jnp.concatenate(
        [rows_qkv.reshape(8, 4, D).transpose(1, 0, 2).reshape(32, D), rows_o], axis=0
    )
    last = spread(last, DP, 8)
    updates = {}
    for index, grad in ((1, wide[:, : 2 * FF]), (3, wide[:, 2 * FF :].reshape(192, D))):
        updates[index] = adam(
            masters[index], grad.astype(F32), firsts[index], seconds[index], rates[index], DECAY
        )
    last, updates[1], updates[3] = tie(last, updates[1], updates[3])
    owned_qkv = last[:, :32].reshape(8, 4, 8, D).transpose(0, 2, 1, 3).reshape(64, 4096)
    owned_o = last[:, 32:].reshape(128, D)
    for index, grad, decay in ((0, owned_qkv, DECAY), (2, owned_o, DECAY), (4, grad_gains, 0.0)):
        updates[index] = adam(
            masters[index], grad.astype(F32), firsts[index], seconds[index], rates[index], decay
        )
    updates[0], updates[2], *blocks = tie(updates[0], updates[2], *blocks)
    total_back = blocks[0].astype(F32)
    for value in blocks[1:]:
        total_back += value.astype(F32)
    hidden_grad = grad_middle + norm_back(total_back, unit_one, factor_one)
    results = [output.astype(BF)[None], hidden_grad[None]]
    for index in range(5):
        results.extend(updates[index])
    return tuple(results)


def solution(mesh):
    fine = Mesh(mesh.devices.reshape(2, 4, 2, 4, 2), ("xlo", "z", "xhi", "y", "core"))
    tokens = P(DP, SEQ, None)
    rows = P(SEQ, None)
    return jax.shard_map(
        on_device,
        mesh=fine,
        in_specs=(tokens, tokens, P(DP, SEQ))
        + (rows, rows, rows, rows, P(SEQ)) * 3,
        out_specs=(tokens, tokens) + (rows,) * 12 + (P(SEQ),) * 3,
        check_vma=False,
    )
```
